128 devices in a mesh: row: 8 (over x_hi, y), col: 16 (over x_lo, z, core).
Axes of the slice: x: 4 (x_hi: 2, x_lo: 2; x = x_hi * 2 + x_lo), y: 4, z: 4, core: 2. Of those that a mesh axis runs over, the one named last changes fastest.
Arguments:
- counts: int32 [16384, 32768], P('row', 'col'), may hold values from 0 to 64
- row_totals: int32 [16384], P('row'), may hold values from 1000 to 90000
- column_totals: int32 [32768], P('col'), may hold values from 1000 to 60000
- row_vectors: float32 [16384, 256], P(('row', 'col')), may hold values from -0.6 to 0.6
- column_vectors: float32 [32768, 256], P(('col', 'row')), may hold values from -0.6 to 0.6
- row_squares: float32 [16384, 256], P(('row', 'col')), may hold values from 327.68 to 3276.8
- column_squares: float32 [32768, 256], P(('col', 'row')), may hold values from 163.84 to 1638.4
Outputs:
- new_rows: float32 [16384, 256], P(('row', 'col'))
- new_columns: float32 [32768, 256], P(('col', 'row'))
- squares_row: float32 [16384, 256], P(('row', 'col'))
- squares_column: float32 [32768, 256], P(('col', 'row'))
- mean_loss: float32 [], replicated
The draws below stay inside these ranges and needn't reach their ends.
All inputs are finite; a program needn't handle non-finite values.
Results may differ from the reference program's by a relative error of at most 0.0047.
Values may be sent and summed in bfloat16 or wider, within the bound.
A program may use at most 128 MiB of HBM per device.

```python
import math
import jax
import jax.numpy as jnp
from jax import lax

K = 256
ROWS_ALL = 16384
COLS_ALL = 32768


def draw_counts(key, part):
    key = jax.random.fold_in(key, 11)
    first, second, third = jax.random.split(key, 3)
    shape = (ROWS_ALL, COLS_ALL)
    live = jax.random.randint(first, shape, 0, 10) < 4
    expo = jax.random.randint(second, shape, 0, 7)
    span = jnp.left_shift(jnp.ones(shape, jnp.int32), expo)
    value = jax.random.randint(third, shape, 0, 64) % span + 1
    return jnp.where(live, value, 0).astype(jnp.int32)


def draw_row_totals(key, part):
    key = jax.random.fold_in(key, 23)
    base = jax.random.randint(key, (ROWS_ALL,), 1000, 30000)
    base = base.at[0].set(1000)
    place = jnp.arange(ROWS_ALL, dtype=jnp.int32)
    factor = 64 + 128 * place // ROWS_ALL
    result = base * factor // 64
    return result.at[ROWS_ALL - 1].set(90000).astype(jnp.int32)


def draw_column_totals(key, part):
    key = jax.random.fold_in(key, 37)
    base = jax.random.randint(key, (COLS_ALL,), 1000, 60000)
    base = base.at[0].set(1000)
    return base.at[COLS_ALL - 1].set(60000).astype(jnp.int32)


def block_levels(key, dims, pieces, least, largest):
    level = 1.0
    for axis_at, parts in pieces:
        heights = jax.random.uniform(jax.random.fold_in(jax.random.fold_in(key, 6), axis_at), (parts,), jnp.float32, least / len(pieces), largest / len(pieces))
        level = level * jnp.repeat(jnp.exp(heights), dims[axis_at] // parts).reshape((-1,) + (1,) * (len(dims) - 1 - axis_at))
    return level


def gaussian(key, shape, scale, reach, cuts=(), held_as=jnp.bfloat16):
    values = jax.random.normal(key, shape, jnp.float32) * scale
    if len(cuts) > 0:
        values = block_levels(key, shape, cuts, -0.22, 0.18) * values
    return jnp.clip(values, min=-reach, max=reach).astype(held_as)


def setup_inputs(seed: int = 0) -> dict:
    seeds = jax.random.split(jax.random.key(seed), 8)
    return {
        "counts": draw_counts(jax.random.fold_in(seeds[7], 71), 0),
        "row_totals": draw_row_totals(jax.random.fold_in(seeds[7], 71), 0),
        "column_totals": draw_column_totals(jax.random.fold_in(seeds[7], 71), 0),
        "row_vectors": gaussian(seeds[3], (ROWS_ALL, K), 0.1, 0.6, ((0, 128),), jnp.float32),
        "column_vectors": gaussian(seeds[4], (COLS_ALL, K), 0.1, 0.6, ((0, 128),), jnp.float32),
        "row_squares": jnp.clip(jnp.exp(math.log(3276.8) - 2.3025851 * jax.random.uniform(seeds[5], (ROWS_ALL, K), jnp.float32) ** block_levels(seeds[5], (ROWS_ALL, K), ((0, 128),), -0.2, 0.2)), 327.68, 3276.8),
        "column_squares": jnp.clip(jnp.exp(math.log(1638.4) - 2.3025851 * jax.random.uniform(seeds[6], (COLS_ALL, K), jnp.float32) ** block_levels(seeds[6], (COLS_ALL, K), ((0, 128),), -0.2, 0.2)), 163.84, 1638.4),
    }


def reference(counts, row_totals, column_totals, row_vectors, column_vectors, row_squares, column_squares):
    high = lax.Precision.HIGHEST
    row_half = row_vectors.astype(jnp.bfloat16).astype(jnp.float32)
    column_half = column_vectors.astype(jnp.bfloat16).astype(jnp.float32)
    log_total = jnp.log(jnp.sum(row_totals.astype(jnp.float32)))
    log_columns = jnp.log(column_totals.astype(jnp.float32))
    height = math.gcd(ROWS_ALL, 256)
    blocks = ROWS_ALL // height

    def visit(carry, index):
        column_grad, loss_total = carry
        start = (index * height).astype(jnp.int32)
        block_counts = lax.dynamic_slice_in_dim(counts, start, height, 0).astype(jnp.float32)
        block_rows = lax.dynamic_slice_in_dim(row_half, start, height, 0)
        block_totals = lax.dynamic_slice_in_dim(row_totals, start, height, 0).astype(jnp.float32)
        scores = jnp.dot(block_rows, column_half.T, precision=high, preferred_element_type=jnp.float32)
        pmi = jnp.log(jnp.maximum(block_counts, 1.0)) + log_total - jnp.log(block_totals)[:, None] - log_columns[None, :]
        offset = scores - pmi
        observed = block_counts > 0.0
        confidence = 0.1 + 0.25 * jnp.sqrt(block_counts)
        term = jnp.where(observed, 0.5 * confidence * offset * offset, jax.nn.softplus(offset))
        slope = jnp.where(observed, confidence * offset, jax.nn.sigmoid(offset))
        slopes = lax.optimization_barrier(slope.astype(jnp.bfloat16)).astype(jnp.float32)
        row_grad = jnp.dot(slopes, column_half, precision=high, preferred_element_type=jnp.float32)
        column_grad = column_grad + jnp.dot(slopes.T, block_rows, precision=high, preferred_element_type=jnp.float32)
        return ((column_grad, loss_total + jnp.sum(term)), row_grad)
    start_carry = (jnp.zeros((COLS_ALL, K), jnp.float32), jnp.zeros((), jnp.float32))
    (column_grad, loss_total), row_grads = lax.scan(visit, start_carry, jnp.arange(blocks, dtype=jnp.int32))
    row_grad = row_grads.reshape(ROWS_ALL, K)
    squares_row = row_squares + row_grad * row_grad
    new_rows = row_vectors - row_grad / jnp.sqrt(squares_row)
    squares_column = column_squares + column_grad * column_grad
    new_columns = column_vectors - column_grad / jnp.sqrt(squares_column)
    mean_loss = loss_total / (ROWS_ALL * COLS_ALL)
    return (new_rows, new_columns, squares_row, squares_column, mean_loss)
```

```python
import jax
import jax.numpy as jnp
from jax import lax
from jax.experimental import pallas as pl
from jax.experimental.pallas import tpu as pltpu
from jax.sharding import PartitionSpec as P

F32 = jnp.float32
BF16 = jnp.bfloat16
LOG2E = 1.4426950408889634
LN2 = 0.6931471805599453
SHIFT = 20
K = 256
NR = 2048
NC = 2048
STRIP = 128
SLOTS = 6
TILE = 512
PIECE = 16

R_PARTNER, R_PLUS, R_MINUS, R_PPLUS, R_PMINUS, R_HA, R_HB, R_PHA, R_PHB, R_SIB, R_PSIB = range(11)
C_PARTNER, C_PLUS, C_MINUS, C_PPLUS, C_PMINUS, C_HA, C_HB, C_PHA, C_PHB = range(11, 20)
G_A, G_B, G_PA, G_PB, G_PPLUS, G_PMINUS, G_PARTNER, G_PLUS, G_MINUS = range(20, 29)
G_SIB = 29
G_ROWS = 30
N_SEMS = 38


def kernel(
    counts, row_totals, column_totals, row_vectors, column_vectors, row_squares, column_squares,
    new_rows, new_columns, squares_row, squares_column, mean_loss,
    cbuf, lrow, lcol, B, C, rows, rowsT, cols, rg, cg, slopes_a, slopes_b, scores_a, scores_b, lacc,
    csend, chalf, cwhole, rsend, rsib, rsum, rpart, small, small_in, small_row, small_col,
    csem, ssem, rsem, small_s, small_r,
):
    r = lax.axis_index("row")
    c = lax.axis_index("col")
    hi, y = r // 4, r % 4
    lo, z, core = c // 8, (c // 2) % 4, c % 2
    chip = lo * 4 + z

    def row_at(h, yy):
        return h * 4 + (yy + 4) % 4

    def col_at(l, zz, k):
        return l * 8 + ((zz + 4) % 4) * 2 + k

    def remote(src, dst, which, dev):
        return pltpu.make_async_remote_copy(
            src_ref=src, dst_ref=dst, send_sem=ssem.at[which], recv_sem=rsem.at[which],
            device_id=dev, device_id_type=pl.DeviceIdType.MESH)

    def strip(i, slot):
        return pltpu.make_async_copy(
            counts.at[pl.ds(pl.multiple_of(i * STRIP, STRIP), STRIP)], cbuf.at[slot], csem.at[slot])

    for s in range(SLOTS):
        strip(s, s).start()

    barrier = pltpu.get_barrier_semaphore()
    for d in range(1, 8):
        pl.semaphore_signal(barrier, inc=1, device_id=((r + d) % 8, c), device_id_type=pl.DeviceIdType.MESH)
    for d in range(1, 16):
        pl.semaphore_signal(barrier, inc=1, device_id=(r, (c + d) % 16), device_id_type=pl.DeviceIdType.MESH)

    rows[lo, z, core] = row_vectors[...].astype(BF16)
    cols[r] = column_vectors[...].astype(BF16)
    part = jnp.sum(row_totals[...].astype(F32), axis=0, keepdims=True)
    small[0] = jnp.broadcast_to(jnp.sum(part, axis=1, keepdims=True), (8, 128))

    pl.semaphore_wait(barrier, 22)

    totals = []
    for d in range(1, 8):
        totals.append(pltpu.make_async_remote_copy(
            src_ref=small.at[0], dst_ref=small_in.at[d], send_sem=small_s.at[d], recv_sem=small_r.at[d],
            device_id=((r + d) % 8, c), device_id_type=pl.DeviceIdType.MESH))
        totals[-1].start()

    zp, zm = (r, col_at(lo, z + 1, core)), (r, col_at(lo, z - 1, core))
    lop = (r, col_at(1 - lo, z, core))
    sib = (r, col_at(lo, z, 1 - core))
    yp, ym = (row_at(hi, y + 1), c), (row_at(hi, y - 1), c)
    hip = (row_at(1 - hi, y), c)
    zn, zl, zf = (z + 1) % 4, (z + 3) % 4, (z + 2) % 4
    rn, rl, rf = row_at(hi, y + 1), row_at(hi, y - 1), row_at(hi, y + 2)
    qh, qn, ql, qf = row_at(1 - hi, y), row_at(1 - hi, y + 1), row_at(1 - hi, y - 1), row_at(1 - hi, y + 2)
    A, Bh = pl.ds(0, 64), pl.ds(64, 64)
    CA, CB = pl.ds(0, 128), pl.ds(128, 128)

    def rblock(l, zz):
        return rows.at[l, zz, core]

    def rcopy(l, zz, which, dev):
        return remote(rblock(l, zz), rblock(l, zz), which, dev)

    def rhalf(l, zz, h, which, dev):
        return remote(rows.at[l, zz, core, h], rows.at[l, zz, core, h], which, dev)

    def ccopy(q, which, dev):
        return remote(cols.at[q], cols.at[q], which, dev)

    def chalfcopy(q, h, which, dev):
        return remote(cols.at[q, h], cols.at[q, h], which, dev)

    sent = []

    def go(copy):
        copy.start()
        sent.append(copy)
        return copy

    c_partner = go(ccopy(r, C_PARTNER, hip))
    r_partner = go(rcopy(lo, z, R_PARTNER, lop))
    r_plus = go(rcopy(lo, z, R_PLUS, zp))
    r_minus = go(rcopy(lo, z, R_MINUS, zm))
    c_plus = go(ccopy(r, C_PLUS, yp))
    c_minus = go(ccopy(r, C_MINUS, ym))

    for b in range(16):
        v = jnp.log(row_totals[b:b + 1, :].astype(F32))
        lrow[b * 128:(b + 1) * 128, :] = jnp.transpose(jnp.broadcast_to(v, (128, 128)))

    grand = small[0]
    for d in range(1, 8):
        totals[d - 1].wait_recv()
        grand = grand + small_in[d]
    log_total = jnp.log(grand[0:1, 0:1])
    lcol[...] = jnp.broadcast_to(jnp.log(column_totals[...].astype(F32)) - log_total, (8, NC))

    def prepare(first, last):
        def one(i, carry):
            slot = i % SLOTS
            strip(i, slot).wait()

            def inner(t, carry):
                t8 = pl.multiple_of(t * 8, 8)
                r0 = pl.multiple_of(i * STRIP + t * 8, 8)
                lr = lrow[pl.ds(r0, 8), :]
                for q in range(NC // 128):
                    at = slice(q * 128, (q + 1) * 128)
                    n = cbuf[slot, pl.ds(t8, 8), at].astype(F32)
                    m = jnp.maximum(n, 1.0)
                    seen = n > 0
                    B[pl.ds(r0, 8), at] = jnp.where(seen, jnp.log(m), SHIFT * LN2) - lr - lcol[:, at]
                    C[pl.ds(r0, 8), at] = jnp.where(seen, (0.25 * n) * lax.rsqrt(m) + 0.1, 0.0)
                return carry

            lax.fori_loop(0, STRIP // 8, inner, 0, unroll=2)

            @pl.when(i + SLOTS < NR // STRIP)
            def _():
                strip(i + SLOTS, slot).start()

            return carry

        lax.fori_loop(first, last, one, 0)

    prepare(0, 4)
    r_plus.wait_recv()
    go(rhalf(lo, zl, A, R_HA, zp))
    r_minus.wait_recv()
    go(rhalf(lo, zn, Bh, R_HB, zm))
    r_partner.wait_recv()
    r_pplus = go(rcopy(1 - lo, z, R_PPLUS, zp))
    r_pminus = go(rcopy(1 - lo, z, R_PMINUS, zm))
    c_plus.wait_recv()
    c_ha = go(chalfcopy(rl, CA, C_HA, yp))
    c_minus.wait_recv()
    c_hb = go(chalfcopy(rn, CB, C_HB, ym))
    prepare(4, 8)
    c_partner.wait_recv()
    c_pplus = go(ccopy(qh, C_PPLUS, yp))
    c_pminus = go(ccopy(qh, C_PMINUS, ym))
    r_pplus.wait_recv()
    go(rhalf(1 - lo, zl, A, R_PHA, zp))
    r_pminus.wait_recv()
    go(rhalf(1 - lo, zn, Bh, R_PHB, zm))
    prepare(8, 12)
    rhalf(lo, zf, A, R_HA, zp).wait_recv()
    rhalf(lo, zf, Bh, R_HB, zm).wait_recv()
    go(remote(rows.at[lo, :, core], rows.at[lo, :, core], R_SIB, sib))
    c_pplus.wait_recv()
    c_pha = go(chalfcopy(ql, CA, C_PHA, yp))
    c_pminus.wait_recv()
    c_phb = go(chalfcopy(qn, CB, C_PHB, ym))
    prepare(12, 16)
    rhalf(1 - lo, zf, A, R_PHA, zp).wait_recv()
    rhalf(1 - lo, zf, Bh, R_PHB, zm).wait_recv()
    go(remote(rows.at[1 - lo, :, core], rows.at[1 - lo, :, core], R_PSIB, sib))
    c_ha.wait_recv()
    c_hb.wait_recv()
    remote(rows.at[lo, :, core], rows.at[lo, :, core], R_SIB, sib).wait_recv()
    remote(rows.at[1 - lo, :, core], rows.at[1 - lo, :, core], R_PSIB, sib).wait_recv()
    c_pha.wait_recv()
    c_phb.wait_recv()

    for l in range(2):
        for zz in range(4):
            for k in range(2):
                at = ((l * 4 + zz) * 2 + k) * 128
                rowsT[:, at:at + 128] = jnp.transpose(rows[l, zz, k].astype(F32)).astype(BF16)

    rg[...] = jnp.zeros_like(rg)
    lacc[...] = jnp.zeros_like(lacc)
    slopes_b[...] = jnp.zeros_like(slopes_b)

    def block_of(j):
        off = jnp.where(j <= 1, 2, jnp.where((j == 2) | (j == 5), 1, jnp.where((j == 3) | (j == 6), 3, 0)))
        h = jnp.where((j == 0) | (j >= 5), hi, 1 - hi)
        return h * 4 + (y + off) % 4

    def row_tile(q):
        n = TILE // 256
        return rows[q // 2, (q % 2) * n:(q % 2 + 1) * n].reshape(TILE, K)

    def do_scores(dst, q, blk):
        dst[...] = lax.dot_general(
            row_tile(q), cols[blk], (((1,), (1,)), ((), ())), preferred_element_type=F32)

    def elementwise(src, dst, q, c0):
        la = jnp.zeros((8, 256), F32)
        lb = jnp.zeros((8, 256), F32)
        for v in range(TILE // PIECE):
            at = slice(v * PIECE, (v + 1) * PIECE)
            ra = q * TILE + v * PIECE
            conf = C[ra:ra + PIECE, pl.ds(c0, 256)]
            x = src[at] - B[ra:ra + PIECE, pl.ds(c0, 256)]
            t = conf * x
            g = jnp.exp2(jnp.where(conf > 0, -1e4, x) * LOG2E)
            d = g + 2.0 ** -SHIFT
            dst[at] = (t + g * pltpu.reciprocal(d, approx=True)).astype(BF16)
            la = la + jnp.sum((t * x).reshape(PIECE // 8, 8, 256), axis=0)
            lb = lb + jnp.sum(jnp.log2(d).reshape(PIECE // 8, 8, 256), axis=0)
        lacc[...] += la * 0.5 + (lb + float(SHIFT * TILE // 8)) * LN2

    def gradients(src, q, blk, slot, first):
        rg[q * TILE:(q + 1) * TILE, :] += jnp.dot(src[...], cols[blk], preferred_element_type=F32)
        p = jnp.dot(rowsT[:, q * TILE:(q + 1) * TILE], src[...], preferred_element_type=F32)
        if first:
            cg[slot] = p
        else:
            cg[slot] += p

    far_a = [remote(csend.at[0, CA], chalf.at[0], G_A, yp), remote(csend.at[0, CB], chalf.at[1], G_B, ym)]
    far_p = [remote(csend.at[1, CA], chalf.at[2], G_PA, yp), remote(csend.at[1, CB], chalf.at[3], G_PB, ym)]
    g_pplus = remote(csend.at[2], cwhole.at[0], G_PPLUS, yp)
    g_pminus = remote(csend.at[3], cwhole.at[1], G_PMINUS, ym)
    g_partner = remote(csend.at[4], cwhole.at[2], G_PARTNER, hip)
    g_plus = remote(csend.at[5], cwhole.at[3], G_PLUS, yp)
    g_minus = remote(csend.at[6], cwhole.at[4], G_MINUS, ym)

    def done0():
        csend[0] = cg[0].astype(BF16)
        far_a[0].start()
        far_a[1].start()

    def done1():
        csend[1] = cg[1].astype(BF16)
        far_p[0].start()
        far_p[1].start()

    def done2():
        far_p[0].wait_recv()
        csend[2, 0:128] = (cg[2, 0:128] + chalf[2].astype(F32)).astype(BF16)
        csend[2, 128:256] = cg[2, 128:256].astype(BF16)
        g_pplus.start()

    def done3():
        far_p[1].wait_recv()
        csend[3, 0:128] = cg[3, 0:128].astype(BF16)
        csend[3, 128:256] = (cg[3, 128:256] + chalf[3].astype(F32)).astype(BF16)
        g_pminus.start()

    def done4():
        g_pplus.wait_recv()
        g_pminus.wait_recv()
        csend[4] = (cg[4] + cwhole[0].astype(F32) + cwhole[1].astype(F32)).astype(BF16)
        g_partner.start()

    def done5():
        far_a[0].wait_recv()
        csend[5, 0:128] = (cg[5, 0:128] + chalf[0].astype(F32)).astype(BF16)
        csend[5, 128:256] = cg[5, 128:256].astype(BF16)
        g_plus.start()

    def done6():
        far_a[1].wait_recv()
        csend[6, 0:128] = cg[6, 0:128].astype(BF16)
        csend[6, 128:256] = (cg[6, 128:256] + chalf[1].astype(F32)).astype(BF16)
        g_minus.start()

    do_scores(scores_a, 0, block_of(0))

    def chunk(j, carry):
        for i, done in enumerate((done0, done1, done2, done3, done4, done5)):
            pl.when(j == i + 2)(done)
        here = block_of(j)
        before = block_of(jnp.maximum(j - 1, 0))
        after = block_of(jnp.minimum(j + 1, 7))
        c0 = pl.multiple_of(here * 256, 256)
        slot = jnp.where(j == 0, 8, j - 1)
        do_scores(scores_b, 1, here)
        elementwise(scores_a, slopes_a, 0, c0)
        gradients(slopes_b, 3, before, slot, False)
        do_scores(scores_a, 2, here)
        elementwise(scores_b, slopes_b, 1, c0)
        gradients(slopes_a, 0, here, j, True)
        do_scores(scores_b, 3, here)
        elementwise(scores_a, slopes_a, 2, c0)
        gradients(slopes_b, 1, here, j, False)
        do_scores(scores_a, 0, after)
        elementwise(scores_b, slopes_b, 3, c0)
        gradients(slopes_a, 2, here, j, False)
        return carry

    cg[8] = jnp.zeros((256, 256), F32)
    lax.fori_loop(0, 8, chunk, 0)
    gradients(slopes_b, 3, r, 7, False)

    g_sib = remote(rsend, rsib, G_SIB, sib)

    def rg_block(p, k):
        return rg[pl.ds(pl.multiple_of((p * 2 + k) * 128, 128), 128), :]

    for p in range(8):
        rsend[p] = rg_block(p, 1 - core).astype(BF16)
    g_sib.start()
    done6()

    small[1] = jnp.broadcast_to(
        jnp.sum(jnp.sum(lacc[...], axis=0, keepdims=True), axis=1, keepdims=True), (8, 128))
    losses = []
    for d in range(1, 8):
        losses.append(pltpu.make_async_remote_copy(
            src_ref=small.at[1], dst_ref=small_row.at[d], send_sem=small_s.at[7 + d], recv_sem=small_r.at[7 + d],
            device_id=((r + d) % 8, c), device_id_type=pl.DeviceIdType.MESH))
        losses[-1].start()

    g_sib.wait_recv()
    row_copies = []
    for d in range(1, 8):
        p = (chip + d) % 8
        rsum[d] = (rg_block(p, core) + rsib[p].astype(F32)).astype(BF16)
        row_copies.append(remote(rsum.at[d], rpart.at[d], G_ROWS + d, (r, p * 2 + core)))
        row_copies[-1].start()

    loss = small[1]
    for d in range(1, 8):
        losses[d - 1].wait_recv()
        loss = loss + small_row[d]
    small[2] = loss
    for d in range(1, 16):
        losses.append(pltpu.make_async_remote_copy(
            src_ref=small.at[2], dst_ref=small_col.at[d], send_sem=small_s.at[14 + d], recv_sem=small_r.at[14 + d],
            device_id=(r, (c + d) % 16), device_id_type=pl.DeviceIdType.MESH))
        losses[-1].start()

    g_partner.wait_recv()
    g_plus.wait_recv()
    g_minus.wait_recv()
    cgrad = cg[7] + cwhole[2].astype(F32) + cwhole[3].astype(F32) + cwhole[4].astype(F32)
    cgrad = jnp.transpose(cgrad)
    csq = column_squares[...] + cgrad * cgrad
    squares_column[...] = csq
    new_columns[...] = column_vectors[...] - cgrad * lax.rsqrt(csq)

    rgrad = rg_block(chip, core) + rsib[chip].astype(F32)
    for d in range(1, 8):
        row_copies[d - 1].wait_recv()
        rgrad = rgrad + rpart[d].astype(F32)
    rsq = row_squares[...] + rgrad * rgrad
    squares_row[...] = rsq
    new_rows[...] = row_vectors[...] - rgrad * lax.rsqrt(rsq)

    loss = small[2]
    for d in range(1, 16):
        losses[6 + d].wait_recv()
        loss = loss + small_col[d]
    mean_loss[...] = loss * (1.0 / 536870912.0)

    for copy in sent + far_a + far_p + [g_pplus, g_pminus, g_partner, g_plus, g_minus, g_sib] + row_copies + totals + losses:
        copy.wait_send()


def on_device(
    counts, row_totals, column_totals, row_vectors, column_vectors, row_squares, column_squares
):
    vmem = pl.BlockSpec(memory_space=pltpu.VMEM)
    outs = pl.pallas_call(
        kernel,
        out_shape=[
            jax.ShapeDtypeStruct((128, K), F32),
            jax.ShapeDtypeStruct((256, K), F32),
            jax.ShapeDtypeStruct((128, K), F32),
            jax.ShapeDtypeStruct((256, K), F32),
            jax.ShapeDtypeStruct((8, 128), F32),
        ],
        in_specs=[pl.BlockSpec(memory_space=pl.ANY)] + [vmem] * 6,
        out_specs=[vmem] * 5,
        scratch_shapes=[
            pltpu.VMEM((SLOTS, STRIP, NC), jnp.int32),
            pltpu.VMEM((NR, 128), F32),
            pltpu.VMEM((8, NC), F32),
            pltpu.VMEM((NR, NC), F32),
            pltpu.VMEM((NR, NC), F32),
            pltpu.VMEM((2, 4, 2, 128, K), BF16),
            pltpu.VMEM((K, NR), BF16),
            pltpu.VMEM((8, 256, K), BF16),
            pltpu.VMEM((NR, K), F32),
            pltpu.VMEM((9, K, 256), F32),
            pltpu.VMEM((TILE, 256), BF16),
            pltpu.VMEM((TILE, 256), BF16),
            pltpu.VMEM((TILE, 256), F32),
            pltpu.VMEM((TILE, 256), F32),
            pltpu.VMEM((8, 256), F32),
            pltpu.VMEM((7, K, 256), BF16),
            pltpu.VMEM((4, 128, 256), BF16),
            pltpu.VMEM((5, K, 256), BF16),
            pltpu.VMEM((8, 128, K), BF16),
            pltpu.VMEM((8, 128, K), BF16),
            pltpu.VMEM((8, 128, K), BF16),
            pltpu.VMEM((8, 128, K), BF16),
            pltpu.VMEM((3, 8, 128), F32),
            pltpu.VMEM((8, 8, 128), F32),
            pltpu.VMEM((8, 8, 128), F32),
            pltpu.VMEM((16, 8, 128), F32),
            pltpu.SemaphoreType.DMA((SLOTS,)),
            pltpu.SemaphoreType.DMA((N_SEMS,)),
            pltpu.SemaphoreType.DMA((N_SEMS,)),
            pltpu.SemaphoreType.DMA((32,)),
            pltpu.SemaphoreType.DMA((32,)),
        ],
        compiler_params=pltpu.CompilerParams(
            collective_id=0, has_side_effects=True, vmem_limit_bytes=63 * 1024 * 1024),
        name="swivel_step",
    )(
        counts,
        row_totals.reshape(16, 128),
        column_totals.reshape(1, NC),
        row_vectors,
        column_vectors,
        row_squares,
        column_squares,
    )
    return outs[0], outs[1], outs[2], outs[3], outs[4][0, 0]


def solution(mesh):
    in_specs = (
        P("row", "col"),
        P("row"),
        P("col"),
        P(("row", "col"), None),
        P(("col", "row"), None),
        P(("row", "col"), None),
        P(("col", "row"), None),
    )
    out_specs = (
        P(("row", "col"), None),
        P(("col", "row"), None),
        P(("row", "col"), None),
        P(("col", "row"), None),
        P(),
    )
    return jax.shard_map(
        on_device, mesh=mesh, in_specs=in_specs, out_specs=out_specs, check_vma=False
    )
```

```python
import jax
import jax.numpy as jnp
from jax import lax
from jax.experimental import pallas as pl
from jax.experimental.pallas import tpu as pltpu
from jax.sharding import PartitionSpec as P

F32 = jnp.float32
BF16 = jnp.bfloat16
LOG2E = 1.4426950408889634
LN2 = 0.6931471805599453
SHIFT = 20
K = 256
NR = 2048
NC = 2048
STRIP = 128
SLOTS = 6
TILE = 512
PIECE = 16

R_PARTNER, R_PLUS, R_MINUS, R_FAR, R_PPLUS, R_PMINUS, R_PFAR, R_OWN, R_SIB, R_PSIB = range(10)
C_PARTNER, C_PLUS, C_MINUS, C_FAR, C_PPLUS, C_PMINUS, C_PFAR = range(10, 17)
G_COLS = 17
G_SIB = 24
G_ROWS = 32
N_SEMS = 40
PHASE1 = 5
PHASE2 = 3


def kernel(
    counts, row_totals, column_totals, row_vectors, column_vectors,
    row_grad, column_grad, mean_loss,
    cbuf, lrow, lcol, B, C, rows, rowsT, cols, colsq, rg, cg, cgq, slopes_a, slopes_b, scores_a, scores_b,
    sq_a, sq_b, tq_a, tq_b, lacc,
    csend, cpart, rsend, rsib, rsum, rpart, small, small_in, small_row, small_col,
    csem, ssem, rsem, small_s, small_r,
):
    r = lax.axis_index("row")
    c = lax.axis_index("col")
    hi, y = r // 4, r % 4
    lo, z, core = c // 8, (c // 2) % 4, c % 2

    def row_at(h, yy):
        return h * 4 + (yy + 4) % 4

    def col_at(l, zz, k):
        return l * 8 + ((zz + 4) % 4) * 2 + k

    def remote(src, dst, which, dev):
        return pltpu.make_async_remote_copy(
            src_ref=src, dst_ref=dst, send_sem=ssem.at[which], recv_sem=rsem.at[which],
            device_id=dev, device_id_type=pl.DeviceIdType.MESH)

    def small_copy(src, dst, which, dev):
        return pltpu.make_async_remote_copy(
            src_ref=src, dst_ref=dst, send_sem=small_s.at[which], recv_sem=small_r.at[which],
            device_id=dev, device_id_type=pl.DeviceIdType.MESH)

    def strip(i, slot):
        return pltpu.make_async_copy(
            counts.at[pl.ds(pl.multiple_of(i * STRIP, STRIP), STRIP)], cbuf.at[slot], csem.at[slot])

    for s in range(SLOTS):
        strip(s, s).start()

    barrier = pltpu.get_barrier_semaphore()
    for d in range(1, 8):
        pl.semaphore_signal(barrier, inc=1, device_id=((r + d) % 8, c), device_id_type=pl.DeviceIdType.MESH)
    for d in range(1, 16):
        pl.semaphore_signal(barrier, inc=1, device_id=(r, (c + d) % 16), device_id_type=pl.DeviceIdType.MESH)

    rows[lo, z, core] = row_vectors[...].astype(BF16)
    cols[r] = column_vectors[...].astype(BF16)
    part = jnp.sum(row_totals[...].astype(F32), axis=0, keepdims=True)
    small[0] = jnp.broadcast_to(jnp.sum(part, axis=1, keepdims=True), (8, 128))
    for b in range(16):
        v = jnp.log(row_totals[b:b + 1, :].astype(F32))
        lrow[b * 128:(b + 1) * 128, :] = jnp.transpose(jnp.broadcast_to(v, (128, 128)))
    lcol[...] = jnp.broadcast_to(jnp.log(column_totals[...].astype(F32)), (8, NC))

    def prepare(first, last):
        def one(i, carry):
            slot = i % SLOTS
            strip(i, slot).wait()

            def inner(t, carry):
                t8 = pl.multiple_of(t * 8, 8)
                r0 = pl.multiple_of(i * STRIP + t * 8, 8)
                lr = lrow[pl.ds(r0, 8), :]
                for q in range(NC // 128):
                    at = slice(q * 128, (q + 1) * 128)
                    n = cbuf[slot, pl.ds(t8, 8), at].astype(F32)
                    m = jnp.maximum(n, 1.0)
                    seen = n > 0
                    B[pl.ds(r0, 8), at] = jnp.where(seen, jnp.log(m), SHIFT * LN2) - lr - lcol[:, at]
                    C[pl.ds(r0, 8), at] = jnp.where(seen, (0.25 * n) * lax.rsqrt(m) + 0.1, 0.0)
                return carry

            lax.fori_loop(0, STRIP // 8, inner, 0, unroll=2)

            @pl.when(i + SLOTS < NR // STRIP)
            def _():
                strip(i + SLOTS, slot).start()

            return carry

        lax.fori_loop(first, last, one, 0)

    prepare(0, 14)
    pl.semaphore_wait(barrier, 22)

    zp, zm, zz2 = (r, col_at(lo, z + 1, core)), (r, col_at(lo, z - 1, core)), (r, col_at(lo, z + 2, core))
    lop = (r, col_at(1 - lo, z, core))
    sib = (r, col_at(lo, z, 1 - core))
    yp, ym, yy2 = (row_at(hi, y + 1), c), (row_at(hi, y - 1), c), (row_at(hi, y + 2), c)
    hip = (row_at(1 - hi, y), c)
    rf = row_at(hi, y + 2)
    qh = row_at(1 - hi, y)

    def rcopy(l, zz, which, dev):
        return remote(rows.at[l, zz, core], rows.at[l, zz, core], which, dev)

    def ccopy(q, which, dev):
        return remote(cols.at[q], cols.at[q], which, dev)

    sent = []

    def go(copy):
        copy.start()
        sent.append(copy)
        return copy

    r_partner = go(rcopy(lo, z, R_PARTNER, lop))
    r_plus = go(rcopy(lo, z, R_PLUS, zp))
    r_minus = go(rcopy(lo, z, R_MINUS, zm))
    r_far = go(rcopy(lo, z, R_FAR, zz2))
    c_partner = go(ccopy(r, C_PARTNER, hip))
    c_plus = go(ccopy(r, C_PLUS, yp))
    c_minus = go(ccopy(r, C_MINUS, ym))
    c_far = go(ccopy(r, C_FAR, yy2))
    totals = []
    for d in range(1, 8):
        totals.append(small_copy(small.at[0], small_in.at[d], d, ((r + d) % 8, c)))
        totals[-1].start()

    prepare(14, 16)
    rg[...] = jnp.zeros_like(rg)
    lacc[...] = jnp.zeros_like(lacc)
    slopes_b[...] = jnp.zeros_like(slopes_b)
    tq_b[...] = jnp.zeros_like(tq_b)
    cg[PHASE1] = jnp.zeros((256, 256), F32)
    cgq[...] = jnp.zeros_like(cgq)

    r_partner.wait_recv()
    r_pplus = go(rcopy(1 - lo, z, R_PPLUS, zp))
    r_pminus = go(rcopy(1 - lo, z, R_PMINUS, zm))
    r_pfar = go(rcopy(1 - lo, z, R_PFAR, zz2))
    r_plus.wait_recv()
    r_minus.wait_recv()
    r_far.wait_recv()
    r_sib = go(remote(rows.at[lo, :, core], rows.at[lo, :, core], R_SIB, sib))
    c_partner.wait_recv()
    c_pplus = go(ccopy(qh, C_PPLUS, yp))
    c_pminus = go(ccopy(qh, C_PMINUS, ym))

    grand = small[0]
    for d in range(1, 8):
        totals[d - 1].wait_recv()
        grand = grand + small_in[d]
    log_total = jnp.log(grand[0:1, 0:1])

    c_far.wait_recv()
    c_pfar = go(ccopy(rf, C_PFAR, hip))
    r_pplus.wait_recv()
    r_pminus.wait_recv()
    r_pfar.wait_recv()
    r_psib = go(remote(rows.at[1 - lo, :, core], rows.at[1 - lo, :, core], R_PSIB, sib))
    c_plus.wait_recv()
    c_minus.wait_recv()
    r_sib.wait_recv()
    r_psib.wait_recv()

    for l in range(2):
        for zz in range(4):
            for k in range(2):
                at = ((l * 4 + zz) * 2 + k) * 128
                rowsT[:, at:at + 128] = jnp.transpose(rows[l, zz, k].astype(F32)).astype(BF16)
    colsq[0:256] = cols[row_at(hi, y + 1)]
    colsq[256:512] = cols[row_at(hi, y - 1)]
    colsq[512:768] = cols[r]

    c_pminus.wait_recv()
    c_pplus.wait_recv()

    def piece(conf, score, base):
        x = score - base
        t = conf * x
        g = jnp.exp2(jnp.where(conf > 0, -1e4, x) * LOG2E)
        d = g + 2.0 ** -SHIFT
        slope = (t + g * pltpu.reciprocal(d, approx=True)).astype(BF16)
        fold = (PIECE // 8, 8, 256)
        return slope, jnp.sum((t * x).reshape(fold), axis=0), jnp.sum(jnp.log2(d).reshape(fold), axis=0)

    def block_of(j):
        off = jnp.where(j == 0, 1, jnp.where(j == 1, 3, jnp.where((j == 2) | (j == 4), 2, 0)))
        return jnp.where(j == 4, hi, 1 - hi) * 4 + (y + off) % 4

    def row_tile(q):
        n = TILE // 256
        return rows[q // 2, (q % 2) * n:(q % 2 + 1) * n].reshape(TILE, K)

    def do_scores(dst, q, blk):
        dst[...] = lax.dot_general(
            row_tile(q), cols[blk], (((1,), (1,)), ((), ())), preferred_element_type=F32) - log_total

    def elementwise(src, dst, q, c0):
        la = jnp.zeros((8, 256), F32)
        lb = jnp.zeros((8, 256), F32)
        for v in range(TILE // PIECE):
            at = slice(v * PIECE, (v + 1) * PIECE)
            ra = q * TILE + v * PIECE
            dst[at], a, b = piece(C[ra:ra + PIECE, pl.ds(c0, 256)], src[at], B[ra:ra + PIECE, pl.ds(c0, 256)])
            la = la + a
            lb = lb + b
        lacc[...] += la * 0.5 + (lb + float(SHIFT * TILE // 8)) * LN2

    def gradients(src, q, blk, slot, first):
        rg[q * TILE:(q + 1) * TILE, :] += jnp.dot(src[...], cols[blk], preferred_element_type=F32)
        p = jnp.dot(rowsT[:, q * TILE:(q + 1) * TILE], src[...], preferred_element_type=F32)
        if first:
            cg[slot] = p
        else:
            cg[slot] += p

    def col_copy(j, dest):
        return remote(csend.at[j], cpart.at[j], G_COLS + j, (dest, c))

    do_scores(scores_a, 0, block_of(0))

    def chunk(j, carry):
        here = block_of(j)
        prev = jnp.maximum(j - 1, 0)
        before = block_of(prev)
        after = block_of(jnp.minimum(j + 1, PHASE1 - 1))
        c0 = pl.multiple_of(here * 256, 256)
        slot = jnp.where(j == 0, PHASE1, prev)
        do_scores(scores_b, 1, here)
        elementwise(scores_a, slopes_a, 0, c0)
        gradients(slopes_b, 3, before, slot, False)

        @pl.when(j > 0)
        def _():
            csend[prev] = cg[prev].astype(BF16)
            col_copy(prev, before).start()

        @pl.when(j == 1)
        def _():
            c_pfar.wait_recv()

        do_scores(scores_a, 2, here)
        elementwise(scores_b, slopes_b, 1, c0)
        gradients(slopes_a, 0, here, j, True)
        do_scores(scores_b, 3, here)
        elementwise(scores_a, slopes_a, 2, c0)
        gradients(slopes_b, 1, here, j, False)
        do_scores(scores_a, 0, after)
        elementwise(scores_b, slopes_b, 3, c0)
        gradients(slopes_a, 2, here, j, False)
        return carry

    lax.fori_loop(0, PHASE1, chunk, 0)

    WIDTH = PHASE2 * 256
    qcols = [row_at(hi, y + 1), row_at(hi, y - 1), r]

    def chip_of(i):
        l = jnp.where((i <= 2) | (i == 4), 1 - lo, lo)
        off = jnp.where((i == 0) | (i == 3), 2, jnp.where((i == 1) | (i == 5), 1, jnp.where((i == 2) | (i == 6), 3, 0)))
        return l * 4 + (z + off) % 4

    def q_scores(dst, p):
        tile = rows[p // 4, p % 4].reshape(256, K)
        dst[...] = lax.dot_general(
            tile, colsq[...], (((1,), (1,)), ((), ())), preferred_element_type=F32) - log_total

    def q_elementwise(src, dst, p):
        la = jnp.zeros((8, 256), F32)
        lb = jnp.zeros((8, 256), F32)
        for h in range(PHASE2):
            c0 = pl.multiple_of(qcols[h] * 256, 256)
            for v in range(256 // PIECE):
                at = slice(v * PIECE, (v + 1) * PIECE)
                to = slice(h * 256, (h + 1) * 256)
                ra = pl.ds(pl.multiple_of(p * 256 + v * PIECE, PIECE), PIECE)
                dst[at, to], a, b = piece(C[ra, pl.ds(c0, 256)], src[at, to], B[ra, pl.ds(c0, 256)])
                la = la + a
                lb = lb + b
        lacc[...] += la * 0.5 + (lb + float(SHIFT * WIDTH // 8)) * LN2

    def q_gradients(src, p):
        at = pl.ds(pl.multiple_of(p * 256, 256), 256)
        rg[at, :] += jnp.dot(src[...], colsq[...], preferred_element_type=F32)
        cgq[...] += jnp.dot(rowsT[:, at], src[...], preferred_element_type=F32)

    def rg_block(p, k):
        return rg[pl.ds(pl.multiple_of((p * 2 + k) * 128, 128), 128), :]

    def sib_copy(i):
        return remote(rsend.at[i], rsib.at[i], G_SIB + i, sib)

    def row_copy(i):
        return remote(rsum.at[i], rpart.at[i], G_ROWS + i, (r, chip_of(i) * 2 + core))

    def to_sibling(i):
        rsend[i] = rg_block(chip_of(i), 1 - core).astype(BF16)
        sib_copy(i).start()

    def to_owner(i):
        sib_copy(i).wait_recv()
        rsum[i] = (rg_block(chip_of(i), core) + rsib[i].astype(F32)).astype(BF16)
        row_copy(i).start()

    gradients(slopes_b, 3, block_of(PHASE1 - 1), PHASE1 - 1, False)
    q_scores(sq_a, chip_of(0))
    csend[PHASE1 - 1] = cg[PHASE1 - 1].astype(BF16)
    col_copy(PHASE1 - 1, block_of(PHASE1 - 1)).start()

    def events(i):
        @pl.when(i >= 2)
        def _():
            to_sibling(i - 2)

        @pl.when(i >= 4)
        def _():
            to_owner(i - 4)

    def pair(m, carry):
        i = m * 2
        events(i)
        q_scores(sq_b, chip_of(i + 1))
        q_elementwise(sq_a, tq_a, chip_of(i))
        q_gradients(tq_b, chip_of(jnp.maximum(i - 1, 0)))
        events(i + 1)
        q_scores(sq_a, chip_of(jnp.minimum(i + 2, 7)))
        q_elementwise(sq_b, tq_b, chip_of(i + 1))
        q_gradients(tq_a, chip_of(i))
        return carry

    lax.fori_loop(0, 4, pair, 0)
    small[1] = jnp.broadcast_to(
        jnp.sum(jnp.sum(lacc[...], axis=0, keepdims=True), axis=1, keepdims=True), (8, 128))
    losses = []
    for d in range(1, 8):
        losses.append(small_copy(small.at[1], small_row.at[d], 7 + d, ((r + d) % 8, c)))
        losses[-1].start()
    to_sibling(6)
    q_gradients(tq_b, chip_of(7))
    csend[5] = cgq[:, 0:256].astype(BF16)
    col_copy(5, row_at(hi, y + 1)).start()
    csend[6] = cgq[:, 256:512].astype(BF16)
    col_copy(6, row_at(hi, y - 1)).start()
    to_sibling(7)
    to_owner(4)
    to_owner(5)
    to_owner(6)

    loss = small[1]
    for d in range(1, 8):
        losses[d - 1].wait_recv()
        loss = loss + small_row[d]
    small[2] = loss
    for d in range(1, 16):
        losses.append(small_copy(small.at[2], small_col.at[d], 14 + d, (r, (c + d) % 16)))
        losses[-1].start()

    sib_copy(7).wait_recv()
    grad = rg_block(lo * 4 + z, core) + rsib[7].astype(F32)
    for i in range(7):
        row_copy(i).wait_recv()
        grad = grad + rpart[i].astype(F32)
    row_grad[...] = grad

    total = cgq[:, 512:768]
    for j in range(7):
        col_copy(j, r if j > 6 else qh).wait_recv()
        total = total + cpart[j].astype(F32)
    column_grad[...] = jnp.transpose(total)

    loss = small[2]
    for d in range(1, 16):
        losses[6 + d].wait_recv()
        loss = loss + small_col[d]
    mean_loss[...] = loss * (1.0 / 536870912.0)

    for copy in sent + totals + losses:
        copy.wait_send()
    for j in range(7):
        col_copy(j, qh).wait_send()
    for i in range(8):
        sib_copy(i).wait_send()
    for i in range(7):
        row_copy(i).wait_send()


def update(
    row_grad, column_grad, loss, row_vectors, column_vectors, row_squares, column_squares,
    new_rows, new_columns, squares_row, squares_column, mean_loss,
):
    g = row_grad[...]
    s = row_squares[...] + g * g
    squares_row[...] = s
    new_rows[...] = row_vectors[...] - g * lax.rsqrt(s)
    g = column_grad[...]
    s = column_squares[...] + g * g
    squares_column[...] = s
    new_columns[...] = column_vectors[...] - g * lax.rsqrt(s)
    mean_loss[0, 0] = loss[0, 0]


def on_device(
    counts, row_totals, column_totals, row_vectors, column_vectors, row_squares, column_squares
):
    vmem = pl.BlockSpec(memory_space=pltpu.VMEM)
    smem = pl.BlockSpec(memory_space=pltpu.SMEM)
    row_grad, column_grad, loss = pl.pallas_call(
        kernel,
        out_shape=[
            jax.ShapeDtypeStruct((128, K), F32),
            jax.ShapeDtypeStruct((256, K), F32),
            jax.ShapeDtypeStruct((8, 128), F32),
        ],
        in_specs=[pl.BlockSpec(memory_space=pl.ANY)] + [vmem] * 4,
        out_specs=[vmem] * 3,
        scratch_shapes=[
            pltpu.VMEM((SLOTS, STRIP, NC), jnp.int32),
            pltpu.VMEM((NR, 128), F32),
            pltpu.VMEM((8, NC), F32),
            pltpu.VMEM((NR, NC), F32),
            pltpu.VMEM((NR, NC), F32),
            pltpu.VMEM((2, 4, 2, 128, K), BF16),
            pltpu.VMEM((K, NR), BF16),
            pltpu.VMEM((8, 256, K), BF16),
            pltpu.VMEM((PHASE2 * 256, K), BF16),
            pltpu.VMEM((NR, K), F32),
            pltpu.VMEM((PHASE1 + 1, K, 256), F32),
            pltpu.VMEM((K, PHASE2 * 256), F32),
            pltpu.VMEM((TILE, 256), BF16),
            pltpu.VMEM((TILE, 256), BF16),
            pltpu.VMEM((TILE, 256), F32),
            pltpu.VMEM((TILE, 256), F32),
            pltpu.VMEM((256, PHASE2 * 256), F32),
            pltpu.VMEM((256, PHASE2 * 256), F32),
            pltpu.VMEM((256, PHASE2 * 256), BF16),
            pltpu.VMEM((256, PHASE2 * 256), BF16),
            pltpu.VMEM((8, 256), F32),
            pltpu.VMEM((7, K, 256), BF16),
            pltpu.VMEM((7, K, 256), BF16),
            pltpu.VMEM((8, 128, K), BF16),
            pltpu.VMEM((8, 128, K), BF16),
            pltpu.VMEM((8, 128, K), BF16),
            pltpu.VMEM((8, 128, K), BF16),
            pltpu.VMEM((3, 8, 128), F32),
            pltpu.VMEM((8, 8, 128), F32),
            pltpu.VMEM((8, 8, 128), F32),
            pltpu.VMEM((16, 8, 128), F32),
            pltpu.SemaphoreType.DMA((SLOTS,)),
            pltpu.SemaphoreType.DMA((N_SEMS,)),
            pltpu.SemaphoreType.DMA((N_SEMS,)),
            pltpu.SemaphoreType.DMA((32,)),
            pltpu.SemaphoreType.DMA((32,)),
        ],
        compiler_params=pltpu.CompilerParams(
            collective_id=0, has_side_effects=True, vmem_limit_bytes=63 * 1024 * 1024),
        name="swivel_step",
    )(counts, row_totals.reshape(16, 128), column_totals.reshape(1, NC), row_vectors, column_vectors)
    outs = pl.pallas_call(
        update,
        out_shape=[
            jax.ShapeDtypeStruct((128, K), F32),
            jax.ShapeDtypeStruct((256, K), F32),
            jax.ShapeDtypeStruct((128, K), F32),
            jax.ShapeDtypeStruct((256, K), F32),
            jax.ShapeDtypeStruct((1, 1), F32),
        ],
        in_specs=[vmem, vmem, smem] + [vmem] * 4,
        out_specs=[vmem] * 4 + [smem],
        name="adagrad_update",
    )(row_grad, column_grad, loss, row_vectors, column_vectors, row_squares, column_squares)
    return outs[0], outs[1], outs[2], outs[3], outs[4].reshape(())


def solution(mesh):
    in_specs = (
        P("row", "col"),
        P("row"),
        P("col"),
        P(("row", "col"), None),
        P(("col", "row"), None),
        P(("row", "col"), None),
        P(("col", "row"), None),
    )
    out_specs = (
        P(("row", "col"), None),
        P(("col", "row"), None),
        P(("row", "col"), None),
        P(("col", "row"), None),
        P(),
    )
    return jax.shard_map(
        on_device, mesh=mesh, in_specs=in_specs, out_specs=out_specs, check_vma=False
    )
```

```python
import jax
import jax.numpy as jnp
from jax import lax
from jax.experimental import pallas as pl
from jax.experimental.pallas import tpu as pltpu
from jax.sharding import PartitionSpec as P

F32 = jnp.float32
BF16 = jnp.bfloat16
LOG2E = 1.4426950408889634
LN2 = 0.6931471805599453
SHIFT = 20
K = 256
NR = 2048
NC = 2048
STRIP = 128
SLOTS = 6
TILE = 512
PIECE = 16

R_PARTNER, R_PLUS, R_MINUS, R_FAR, R_PPLUS, R_PMINUS, R_PFAR, R_SPARE, R_SIB, R_PSIB = range(10)
C_PARTNER, C_PLUS, C_MINUS, C_FAR, C_PPLUS, C_PMINUS, C_PFAR = range(10, 17)
G_COLS = 17
G_SIB = 24
G_ROWS = 32
N_SEMS = 40
WIDTH = 768
OWN, NEXT, LAST, CROSS, FAR, CROSS_NEXT, CROSS_LAST, CROSS_FAR = range(8)


def kernel(
    counts, row_totals, column_totals, row_vectors, column_vectors,
    row_grad, column_grad, mean_loss,
    cbuf, lrow, lcol, B, C, rows, rowsT, cols, colsq, rg, cg, cgq, slopes_a, slopes_b, scores_a, scores_b,
    sq_a, sq_b, tq_a, tq_b, lacc,
    csend, cpart, rsend, rsib, rsum, rpart, small, small_in, small_row, small_col,
    csem, ssem, rsem, small_s, small_r,
):
    r = lax.axis_index("row")
    c = lax.axis_index("col")
    hi, y = r // 4, r % 4
    lo, z, core = c // 8, (c // 2) % 4, c % 2

    def row_at(h, yy):
        return h * 4 + (yy + 4) % 4

    def col_at(l, zz, k):
        return l * 8 + ((zz + 4) % 4) * 2 + k

    def remote(src, dst, which, dev):
        return pltpu.make_async_remote_copy(
            src_ref=src, dst_ref=dst, send_sem=ssem.at[which], recv_sem=rsem.at[which],
            device_id=dev, device_id_type=pl.DeviceIdType.MESH)

    def small_copy(src, dst, which, dev):
        return pltpu.make_async_remote_copy(
            src_ref=src, dst_ref=dst, send_sem=small_s.at[which], recv_sem=small_r.at[which],
            device_id=dev, device_id_type=pl.DeviceIdType.MESH)

    def strip(i, slot):
        return pltpu.make_async_copy(
            counts.at[pl.ds(pl.multiple_of(i * STRIP, STRIP), STRIP)], cbuf.at[slot], csem.at[slot])

    for s in range(SLOTS):
        strip(s, s).start()

    barrier = pltpu.get_barrier_semaphore()
    for d in range(1, 8):
        pl.semaphore_signal(barrier, inc=1, device_id=((r + d) % 8, c), device_id_type=pl.DeviceIdType.MESH)
    for d in range(1, 16):
        pl.semaphore_signal(barrier, inc=1, device_id=(r, (c + d) % 16), device_id_type=pl.DeviceIdType.MESH)

    rows[lo, z, core] = row_vectors[...].astype(BF16)
    cols[r] = column_vectors[...].astype(BF16)
    part = jnp.sum(row_totals[...].astype(F32), axis=0, keepdims=True)
    small[0] = jnp.broadcast_to(jnp.sum(part, axis=1, keepdims=True), (8, 128))
    for b in range(16):
        v = jnp.log(row_totals[b:b + 1, :].astype(F32))
        lrow[b * 128:(b + 1) * 128, :] = jnp.transpose(jnp.broadcast_to(v, (128, 128)))
    lcol[...] = jnp.broadcast_to(jnp.log(column_totals[...].astype(F32)), (8, NC))

    def prepare(first, last):
        def one(i, carry):
            slot = i % SLOTS
            strip(i, slot).wait()

            def inner(t, carry):
                t8 = pl.multiple_of(t * 8, 8)
                r0 = pl.multiple_of(i * STRIP + t * 8, 8)
                lr = lrow[pl.ds(r0, 8), :]
                for q in range(NC // 128):
                    at = slice(q * 128, (q + 1) * 128)
                    n = cbuf[slot, pl.ds(t8, 8), at].astype(F32)
                    m = jnp.maximum(n, 1.0)
                    seen = n > 0
                    B[pl.ds(r0, 8), at] = jnp.where(seen, jnp.log(m), SHIFT * LN2) - lr - lcol[:, at]
                    C[pl.ds(r0, 8), at] = jnp.where(seen, (0.25 * n) * lax.rsqrt(m) + 0.1, 0.0)
                return carry

            lax.fori_loop(0, STRIP // 8, inner, 0, unroll=2)

            @pl.when(i + SLOTS < NR // STRIP)
            def _():
                strip(i + SLOTS, slot).start()

            return carry

        lax.fori_loop(first, last, one, 0)

    prepare(0, 14)
    pl.semaphore_wait(barrier, 22)

    zp, zm, zz2 = (r, col_at(lo, z + 1, core)), (r, col_at(lo, z - 1, core)), (r, col_at(lo, z + 2, core))
    lop = (r, col_at(1 - lo, z, core))
    sib = (r, col_at(lo, z, 1 - core))
    yp, ym, yy2 = (row_at(hi, y + 1), c), (row_at(hi, y - 1), c), (row_at(hi, y + 2), c)
    hip = (row_at(1 - hi, y), c)
    rf = row_at(hi, y + 2)
    qh = row_at(1 - hi, y)

    def rcopy(l, zz, which, dev):
        return remote(rows.at[l, zz, core], rows.at[l, zz, core], which, dev)

    def ccopy(q, which, dev):
        return remote(cols.at[q], cols.at[q], which, dev)

    sent = []

    def go(copy):
        copy.start()
        sent.append(copy)
        return copy

    r_partner = go(rcopy(lo, z, R_PARTNER, lop))
    r_plus = go(rcopy(lo, z, R_PLUS, zp))
    r_minus = go(rcopy(lo, z, R_MINUS, zm))
    r_far = go(rcopy(lo, z, R_FAR, zz2))
    c_partner = go(ccopy(r, C_PARTNER, hip))
    c_plus = go(ccopy(r, C_PLUS, yp))
    c_minus = go(ccopy(r, C_MINUS, ym))
    c_far = go(ccopy(r, C_FAR, yy2))
    totals = []
    for d in range(1, 8):
        totals.append(small_copy(small.at[0], small_in.at[d], d, ((r + d) % 8, c)))
        totals[-1].start()

    prepare(14, 16)
    rg[...] = jnp.zeros_like(rg)
    lacc[...] = jnp.zeros_like(lacc)
    slopes_b[...] = jnp.zeros_like(slopes_b)
    cg[...] = jnp.zeros_like(cg)

    r_partner.wait_recv()
    r_pplus = go(rcopy(1 - lo, z, R_PPLUS, zp))
    r_pminus = go(rcopy(1 - lo, z, R_PMINUS, zm))
    r_pfar = go(rcopy(1 - lo, z, R_PFAR, zz2))
    r_plus.wait_recv()
    r_minus.wait_recv()
    r_far.wait_recv()
    r_sib = go(remote(rows.at[lo, :, core], rows.at[lo, :, core], R_SIB, sib))
    c_partner.wait_recv()
    c_pplus = go(ccopy(qh, C_PPLUS, yp))
    c_pminus = go(ccopy(qh, C_PMINUS, ym))

    c_pfar = ccopy(rf, C_PFAR, hip)
    r_psib = remote(rows.at[1 - lo, :, core], rows.at[1 - lo, :, core], R_PSIB, sib)

    grand = small[0]
    for d in range(1, 8):
        totals[d - 1].wait_recv()
        grand = grand + small_in[d]
    log_total = jnp.log(grand[0:1, 0:1])

    def turn_rows(l):
        for zz in range(4):
            for k in range(2):
                at = pl.ds(pl.multiple_of(l * 1024 + (zz * 2 + k) * 128, 128), 128)
                rowsT[:, at] = jnp.transpose(rows[l, zz, k].astype(F32)).astype(BF16)

    r_sib.wait_recv()
    turn_rows(lo)

    def piece(conf, score, base):
        x = score - base
        t = conf * x
        g = jnp.exp2(jnp.where(conf > 0, -1e4, x) * LOG2E)
        d = g + 2.0 ** -SHIFT
        slope = (t + g * pltpu.reciprocal(d, approx=True)).astype(BF16)
        fold = (PIECE // 8, 8, 256)
        return slope, jnp.sum((t * x).reshape(fold), axis=0), jnp.sum(jnp.log2(d).reshape(fold), axis=0)

    def kind_of(u):
        return jnp.where((u == 0) | (u == 3), CROSS, jnp.where((u == 1) | (u == 2), FAR, jnp.where(u <= 6, u - 4, 5 + (u - 7) // 2)))

    def plane_of(u):
        return jnp.where((u <= 1) | ((u >= 8) & (u % 2 == 0)), lo, 1 - lo)

    def block_of(kind):
        off = jnp.where((kind == NEXT) | (kind == CROSS_NEXT), 1, jnp.where(
            (kind == LAST) | (kind == CROSS_LAST), 3, jnp.where((kind == FAR) | (kind == CROSS_FAR), 2, 0)))
        h = jnp.where((kind <= LAST) | (kind == FAR), hi, 1 - hi)
        return h * 4 + (y + off) % 4

    def row_base(l, q):
        return pl.multiple_of(l * 1024 + q * TILE, TILE)

    def do_scores(dst, l, q, blk):
        tile = rows[l, 2 * q:2 * q + 2].reshape(TILE, K)
        dst[...] = lax.dot_general(
            tile, cols[blk], (((1,), (1,)), ((), ())), preferred_element_type=F32) - log_total

    def elementwise(src, dst, l, q, c0):
        la = jnp.zeros((8, 256), F32)
        lb = jnp.zeros((8, 256), F32)
        for v in range(TILE // PIECE):
            at = slice(v * PIECE, (v + 1) * PIECE)
            ra = pl.ds(pl.multiple_of(l * 1024 + q * TILE + v * PIECE, PIECE), PIECE)
            dst[at], a, b = piece(C[ra, pl.ds(c0, 256)], src[at], B[ra, pl.ds(c0, 256)])
            la = la + a
            lb = lb + b
        lacc[...] += la * 0.5 + (lb + float(SHIFT * TILE // 8)) * LN2

    def gradients(src, l, q, blk, kind):
        at = pl.ds(row_base(l, q), TILE)
        rg[at, :] += jnp.dot(src[...], cols[blk], preferred_element_type=F32)
        cg[kind] += jnp.dot(rowsT[:, at], src[...], preferred_element_type=F32)

    S_FAR, S_NEXT_RELAY, S_LAST_RELAY, S_CROSS_FAR, S_CROSS, S_NEXT, S_LAST = range(7)
    col_dest = [rf, row_at(hi, y + 1), row_at(hi, y - 1), row_at(1 - hi, y + 2), qh, row_at(hi, y + 1), row_at(hi, y - 1)]

    def col_copy(j):
        return remote(csend.at[j], cpart.at[j], G_COLS + j, (col_dest[j], c))

    def send_cols(j, value):
        csend[j] = value.astype(BF16)
        col_copy(j).start()

    OFFS = (2, 1, 3, 0)

    def rg_block(l, off, k):
        p = l * 4 + (z + off) % 4
        return rg[pl.ds(pl.multiple_of((p * 2 + k) * 128, 128), 128), :]

    sib_batch = remote(rsend.at[0:4], rsib.at[0:4], G_SIB, sib)

    def sib_copy(i):
        return remote(rsend.at[i], rsib.at[i], G_SIB + i, sib)

    def row_copy(i):
        dev = lop if i == 3 else (r, col_at(lo, z + OFFS[i % 4], core))
        return remote(rsum.at[i], rpart.at[i], G_ROWS + i, dev)

    def send_rows(i, value):
        rsum[i] = value.astype(BF16)
        row_copy(i).start()

    do_scores(scores_a, lo, 0, block_of(CROSS))

    def step(u, carry):
        kind, l = kind_of(u), plane_of(u)
        blk = block_of(kind)
        c0 = pl.multiple_of(blk * 256, 256)
        pu = jnp.maximum(u - 1, 0)
        pkind, plane = kind_of(pu), plane_of(pu)
        nu = jnp.minimum(u + 1, 12)

        @pl.when(u == 0)
        def _():
            c_far.wait_recv()
            c_pfar.start()
            r_pplus.wait_recv()
            r_pminus.wait_recv()
            r_pfar.wait_recv()
            r_psib.start()

        @pl.when(u == 1)
        def _():
            r_psib.wait_recv()
            turn_rows(1 - lo)

        @pl.when(u == 4)
        def _():
            c_plus.wait_recv()
            c_minus.wait_recv()

        @pl.when(u == 6)
        def _():
            c_pminus.wait_recv()

        @pl.when(u == 8)
        def _():
            c_pplus.wait_recv()

        @pl.when(u == 10)
        def _():
            c_pfar.wait_recv()

        do_scores(scores_b, l, 1, blk)
        elementwise(scores_a, slopes_a, l, 0, c0)
        gradients(slopes_b, plane, 1, block_of(pkind), pkind)

        @pl.when(u == 3)
        def _():
            send_cols(S_FAR, cg[FAR])

        @pl.when(u == 9)
        def _():
            send_cols(S_NEXT_RELAY, cg[CROSS_NEXT])

        @pl.when(u == 11)
        def _():
            send_cols(S_LAST_RELAY, cg[CROSS_LAST])

        @pl.when(u == 12)
        def _():
            for i in range(4):
                rsend[i] = rg_block(1 - lo, OFFS[i], 1 - core).astype(BF16)
            sib_batch.start()

        do_scores(scores_a, plane_of(nu), 0, block_of(kind_of(nu)))
        elementwise(scores_b, slopes_b, l, 1, c0)
        gradients(slopes_a, l, 0, blk, kind)
        return carry

    lax.fori_loop(0, 13, step, 0)

    qcols = [r, row_at(hi, y + 1), row_at(hi, y - 1)]
    for h in range(3):
        colsq[h * 256:(h + 1) * 256] = cols[qcols[h]]
        cgq[:, h * 256:(h + 1) * 256] = cg[h]

    def chip_of(t):
        off = jnp.where(t == 0, 2, jnp.where(t == 1, 1, jnp.where(t == 2, 3, 0)))
        return (z + off) % 4

    def q_rows(t, v, size):
        return pl.ds(pl.multiple_of(lo * 1024 + chip_of(t) * 256 + v, size), size)

    def q_scores(dst, t):
        tile = rows[lo, chip_of(t)].reshape(256, K)
        dst[...] = lax.dot_general(
            tile, colsq[...], (((1,), (1,)), ((), ())), preferred_element_type=F32) - log_total

    def q_elementwise(src, dst, t):
        la = jnp.zeros((8, 256), F32)
        lb = jnp.zeros((8, 256), F32)
        for h in range(3):
            c0 = pl.multiple_of(qcols[h] * 256, 256)
            for v in range(256 // PIECE):
                at = slice(v * PIECE, (v + 1) * PIECE)
                to = slice(h * 256, (h + 1) * 256)
                ra = q_rows(t, v * PIECE, PIECE)
                dst[at, to], a, b = piece(C[ra, pl.ds(c0, 256)], src[at, to], B[ra, pl.ds(c0, 256)])
                la = la + a
                lb = lb + b
        lacc[...] += la * 0.5 + (lb + float(SHIFT * WIDTH // 8)) * LN2

    def q_gradients(src, t):
        at = q_rows(t, 0, 256)
        rg[at, :] += jnp.dot(src[...], colsq[...], preferred_element_type=F32)
        cgq[...] += jnp.dot(rowsT[:, at], src[...], preferred_element_type=F32)

    def to_sibling(t):
        rsend[4 + t] = rg_block(lo, OFFS[t], 1 - core).astype(BF16)
        sib_copy(4 + t).start()

    def to_owner(t):
        sib_copy(4 + t).wait_recv()
        send_rows(4 + t, rg_block(lo, OFFS[t], core) + rsib[4 + t].astype(F32))

    gradients(slopes_b, lo, 1, block_of(CROSS_FAR), CROSS_FAR)
    q_scores(sq_a, 0)
    send_cols(S_CROSS_FAR, cg[CROSS_FAR])
    sib_batch.wait_recv()
    for i in range(3):
        send_rows(i, rg_block(1 - lo, OFFS[i], core) + rsib[i].astype(F32))

    q_scores(sq_b, 1)
    q_elementwise(sq_a, tq_a, 0)
    q_scores(sq_a, 2)
    q_elementwise(sq_b, tq_b, 1)
    q_gradients(tq_a, 0)
    to_sibling(0)
    q_scores(sq_b, 3)
    q_elementwise(sq_a, tq_a, 2)
    q_gradients(tq_b, 1)
    to_sibling(1)
    to_owner(0)
    q_elementwise(sq_b, tq_b, 3)
    q_gradients(tq_a, 2)
    to_sibling(2)
    to_owner(1)
    small[1] = jnp.broadcast_to(
        jnp.sum(jnp.sum(lacc[...], axis=0, keepdims=True), axis=1, keepdims=True), (8, 128))
    losses = []
    for d in range(1, 8):
        losses.append(small_copy(small.at[1], small_row.at[d], 7 + d, ((r + d) % 8, c)))
        losses[-1].start()
    q_gradients(tq_b, 3)
    send_cols(S_NEXT, cgq[:, 256:512])
    send_cols(S_LAST, cgq[:, 512:768])
    to_sibling(3)
    to_owner(2)

    col_copy(S_NEXT_RELAY).wait_recv()
    col_copy(S_LAST_RELAY).wait_recv()
    send_cols(S_CROSS, cg[CROSS] + cpart[S_NEXT_RELAY].astype(F32) + cpart[S_LAST_RELAY].astype(F32))
    grad = rg_block(1 - lo, 0, core) + rsib[3].astype(F32)
    for i in range(3):
        row_copy(i).wait_recv()
        grad = grad + rpart[i].astype(F32)
    send_rows(3, grad)

    loss = small[1]
    for d in range(1, 8):
        losses[d - 1].wait_recv()
        loss = loss + small_row[d]
    small[2] = loss
    for d in range(1, 16):
        losses.append(small_copy(small.at[2], small_col.at[d], 14 + d, (r, (c + d) % 16)))
        losses[-1].start()

    sib_copy(7).wait_recv()
    grad = rg_block(lo, 0, core) + rsib[7].astype(F32)
    for i in range(4, 7):
        row_copy(i).wait_recv()
        grad = grad + rpart[i].astype(F32)
    total = cgq[:, 0:256]
    for j in (S_FAR, S_NEXT, S_LAST, S_CROSS_FAR, S_CROSS):
        col_copy(j).wait_recv()
        total = total + cpart[j].astype(F32)
    column_grad[...] = jnp.transpose(total)
    row_copy(3).wait_recv()
    row_grad[...] = grad + rpart[3].astype(F32)

    loss = small[2]
    for d in range(1, 16):
        losses[6 + d].wait_recv()
        loss = loss + small_col[d]
    mean_loss[...] = loss * (1.0 / 536870912.0)

    for copy in sent + totals + losses + [c_pfar, r_psib, sib_batch]:
        copy.wait_send()
    for j in range(7):
        col_copy(j).wait_send()
    for i in range(4, 8):
        sib_copy(i).wait_send()
    for i in range(7):
        row_copy(i).wait_send()


def update(
    row_grad, column_grad, loss, row_vectors, column_vectors, row_squares, column_squares,
    new_rows, new_columns, squares_row, squares_column, mean_loss,
):
    g = row_grad[...]
    s = row_squares[...] + g * g
    squares_row[...] = s
    new_rows[...] = row_vectors[...] - g * lax.rsqrt(s)
    g = column_grad[...]
    s = column_squares[...] + g * g
    squares_column[...] = s
    new_columns[...] = column_vectors[...] - g * lax.rsqrt(s)
    mean_loss[0, 0] = loss[0, 0]


def on_device(
    counts, row_totals, column_totals, row_vectors, column_vectors, row_squares, column_squares
):
    vmem = pl.BlockSpec(memory_space=pltpu.VMEM)
    smem = pl.BlockSpec(memory_space=pltpu.SMEM)
    row_grad, column_grad, loss = pl.pallas_call(
        kernel,
        out_shape=[
            jax.ShapeDtypeStruct((128, K), F32),
            jax.ShapeDtypeStruct((256, K), F32),
            jax.ShapeDtypeStruct((8, 128), F32),
        ],
        in_specs=[pl.BlockSpec(memory_space=pl.ANY)] + [vmem] * 4,
        out_specs=[vmem] * 3,
        scratch_shapes=[
            pltpu.VMEM((SLOTS, STRIP, NC), jnp.int32),
            pltpu.VMEM((NR, 128), F32),
            pltpu.VMEM((8, NC), F32),
            pltpu.VMEM((NR, NC), F32),
            pltpu.VMEM((NR, NC), F32),
            pltpu.VMEM((2, 4, 2, 128, K), BF16),
            pltpu.VMEM((K, NR), BF16),
            pltpu.VMEM((8, 256, K), BF16),
            pltpu.VMEM((WIDTH, K), BF16),
            pltpu.VMEM((NR, K), F32),
            pltpu.VMEM((8, K, 256), F32),
            pltpu.VMEM((K, WIDTH), F32),
            pltpu.VMEM((TILE, 256), BF16),
            pltpu.VMEM((TILE, 256), BF16),
            pltpu.VMEM((TILE, 256), F32),
            pltpu.VMEM((TILE, 256), F32),
            pltpu.VMEM((256, WIDTH), F32),
            pltpu.VMEM((256, WIDTH), F32),
            pltpu.VMEM((256, WIDTH), BF16),
            pltpu.VMEM((256, WIDTH), BF16),
            pltpu.VMEM((8, 256), F32),
            pltpu.VMEM((7, K, 256), BF16),
            pltpu.VMEM((7, K, 256), BF16),
            pltpu.VMEM((8, 128, K), BF16),
            pltpu.VMEM((8, 128, K), BF16),
            pltpu.VMEM((8, 128, K), BF16),
            pltpu.VMEM((8, 128, K), BF16),
            pltpu.VMEM((3, 8, 128), F32),
            pltpu.VMEM((8, 8, 128), F32),
            pltpu.VMEM((8, 8, 128), F32),
            pltpu.VMEM((16, 8, 128), F32),
            pltpu.SemaphoreType.DMA((SLOTS,)),
            pltpu.SemaphoreType.DMA((N_SEMS,)),
            pltpu.SemaphoreType.DMA((N_SEMS,)),
            pltpu.SemaphoreType.DMA((32,)),
            pltpu.SemaphoreType.DMA((32,)),
        ],
        compiler_params=pltpu.CompilerParams(
            collective_id=0, has_side_effects=True, vmem_limit_bytes=63 * 1024 * 1024),
        name="swivel_step",
    )(counts, row_totals.reshape(16, 128), column_totals.reshape(1, NC), row_vectors, column_vectors)
    outs = pl.pallas_call(
        update,
        out_shape=[
            jax.ShapeDtypeStruct((128, K), F32),
            jax.ShapeDtypeStruct((256, K), F32),
            jax.ShapeDtypeStruct((128, K), F32),
            jax.ShapeDtypeStruct((256, K), F32),
            jax.ShapeDtypeStruct((1, 1), F32),
        ],
        in_specs=[vmem, vmem, smem] + [vmem] * 4,
        out_specs=[vmem] * 4 + [smem],
        name="adagrad_update",
    )(row_grad, column_grad, loss, row_vectors, column_vectors, row_squares, column_squares)
    return outs[0], outs[1], outs[2], outs[3], outs[4].reshape(())


def solution(mesh):
    in_specs = (
        P("row", "col"),
        P("row"),
        P("col"),
        P(("row", "col"), None),
        P(("col", "row"), None),
        P(("row", "col"), None),
        P(("col", "row"), None),
    )
    out_specs = (
        P(("row", "col"), None),
        P(("col", "row"), None),
        P(("row", "col"), None),
        P(("col", "row"), None),
        P(),
    )
    return jax.shard_map(
        on_device, mesh=mesh, in_specs=in_specs, out_specs=out_specs, check_vma=False
    )
```

```python
import jax
import jax.numpy as jnp
from jax import lax
from jax.experimental import pallas as pl
from jax.experimental.pallas import tpu as pltpu
from jax.sharding import PartitionSpec as P

F32 = jnp.float32
BF16 = jnp.bfloat16
LOG2E = 1.4426950408889634
LN2 = 0.6931471805599453
SHIFT = 20
K = 256
NR = 2048
NC = 2048
STRIP = 128
SLOTS = 6
TILE = 512
PIECE = 16

R_PARTNER, R_PLUS, R_MINUS, R_FAR, R_PPLUS, R_PMINUS, R_PFAR, R_SPARE, R_SIB, R_PSIB = range(10)
C_PARTNER, C_PLUS, C_MINUS, C_FAR, C_PPLUS, C_PMINUS, C_PFAR = range(10, 17)
G_COLS = 17
G_SIB = 24
G_ROWS = 32
N_SEMS = 40
WIDTH = 768
OWN, NEXT, LAST, CROSS, FAR, CROSS_NEXT, CROSS_LAST, CROSS_FAR = range(8)


def kernel(
    counts, row_totals, column_totals, row_vectors, column_vectors,
    row_grad, column_grad, mean_loss,
    cbuf, lrow, lcol, B, C, rows, rowsT, cols, colsq, rg, cg, cgq, slopes_a, slopes_b, scores_a, scores_b,
    sq_a, sq_b, tq_a, tq_b, lacc,
    csend, cpart, rsend, rsib, rsum, rpart, small, small_in, small_row, small_col,
    csem, ssem, rsem, small_s, small_r,
):
    r = lax.axis_index("row")
    c = lax.axis_index("col")
    hi, y = r // 4, r % 4
    lo, z, core = c // 8, (c // 2) % 4, c % 2

    def row_at(h, yy):
        return h * 4 + (yy + 4) % 4

    def col_at(l, zz, k):
        return l * 8 + ((zz + 4) % 4) * 2 + k

    def remote(src, dst, which, dev):
        return pltpu.make_async_remote_copy(
            src_ref=src, dst_ref=dst, send_sem=ssem.at[which], recv_sem=rsem.at[which],
            device_id=dev, device_id_type=pl.DeviceIdType.MESH)

    def small_copy(src, dst, which, dev):
        return pltpu.make_async_remote_copy(
            src_ref=src, dst_ref=dst, send_sem=small_s.at[which], recv_sem=small_r.at[which],
            device_id=dev, device_id_type=pl.DeviceIdType.MESH)

    def strip(i, slot):
        return pltpu.make_async_copy(
            counts.at[pl.ds(pl.multiple_of(i * STRIP, STRIP), STRIP)], cbuf.at[slot], csem.at[slot])

    for s in range(SLOTS):
        strip(s, s).start()

    barrier = pltpu.get_barrier_semaphore()
    for d in range(1, 8):
        pl.semaphore_signal(barrier, inc=1, device_id=((r + d) % 8, c), device_id_type=pl.DeviceIdType.MESH)
    for d in range(1, 16):
        pl.semaphore_signal(barrier, inc=1, device_id=(r, (c + d) % 16), device_id_type=pl.DeviceIdType.MESH)

    rows[lo, z, core] = row_vectors[...].astype(BF16)
    cols[r] = column_vectors[...].astype(BF16)
    part = jnp.sum(row_totals[...].astype(F32), axis=0, keepdims=True)
    small[0] = jnp.broadcast_to(jnp.sum(part, axis=1, keepdims=True), (8, 128))
    for b in range(16):
        v = jnp.log(row_totals[b:b + 1, :].astype(F32))
        lrow[b * 128:(b + 1) * 128, :] = jnp.transpose(jnp.broadcast_to(v, (128, 128)))
    lcol[...] = jnp.broadcast_to(jnp.log(column_totals[...].astype(F32)), (8, NC))

    def prepare(first, last):
        def one(i, carry):
            slot = i % SLOTS
            strip(i, slot).wait()

            def inner(t, carry):
                t8 = pl.multiple_of(t * 8, 8)
                r0 = pl.multiple_of(i * STRIP + t * 8, 8)
                lr = lrow[pl.ds(r0, 8), :]
                for q in range(NC // 128):
                    at = slice(q * 128, (q + 1) * 128)
                    n = cbuf[slot, pl.ds(t8, 8), at].astype(F32)
                    m = jnp.maximum(n, 1.0)
                    seen = n > 0
                    B[pl.ds(r0, 8), at] = jnp.where(seen, jnp.log(m), SHIFT * LN2) - lr - lcol[:, at]
                    C[pl.ds(r0, 8), at] = jnp.where(seen, (0.25 * n) * lax.rsqrt(m) + 0.1, 0.0)
                return carry

            lax.fori_loop(0, STRIP // 8, inner, 0, unroll=2)

            @pl.when(i + SLOTS < NR // STRIP)
            def _():
                strip(i + SLOTS, slot).start()

            return carry

        lax.fori_loop(first, last, one, 0)

    prepare(0, 11)
    pl.semaphore_wait(barrier, 22)

    zp, zm, zz2 = (r, col_at(lo, z + 1, core)), (r, col_at(lo, z - 1, core)), (r, col_at(lo, z + 2, core))
    lop = (r, col_at(1 - lo, z, core))
    sib = (r, col_at(lo, z, 1 - core))
    yp, ym, yy2 = (row_at(hi, y + 1), c), (row_at(hi, y - 1), c), (row_at(hi, y + 2), c)
    hip = (row_at(1 - hi, y), c)
    rf = row_at(hi, y + 2)
    qh = row_at(1 - hi, y)

    def rcopy(l, zz, which, dev):
        return remote(rows.at[l, zz, core], rows.at[l, zz, core], which, dev)

    def ccopy(q, which, dev):
        return remote(cols.at[q], cols.at[q], which, dev)

    sent = []

    def go(copy):
        copy.start()
        sent.append(copy)
        return copy

    r_partner = go(rcopy(lo, z, R_PARTNER, lop))
    r_plus = go(rcopy(lo, z, R_PLUS, zp))
    r_minus = go(rcopy(lo, z, R_MINUS, zm))
    r_far = go(rcopy(lo, z, R_FAR, zz2))
    c_partner = go(ccopy(r, C_PARTNER, hip))
    c_plus = go(ccopy(r, C_PLUS, yp))
    c_minus = go(ccopy(r, C_MINUS, ym))
    c_far = go(ccopy(r, C_FAR, yy2))
    totals = []
    for d in range(1, 8):
        totals.append(small_copy(small.at[0], small_in.at[d], d, ((r + d) % 8, c)))
        totals[-1].start()

    prepare(11, 16)
    rg[...] = jnp.zeros_like(rg)
    lacc[...] = jnp.zeros_like(lacc)
    slopes_b[...] = jnp.zeros_like(slopes_b)
    cg[...] = jnp.zeros_like(cg)

    r_partner.wait_recv()
    r_pplus = go(rcopy(1 - lo, z, R_PPLUS, zp))
    r_pminus = go(rcopy(1 - lo, z, R_PMINUS, zm))
    r_pfar = go(rcopy(1 - lo, z, R_PFAR, zz2))
    r_plus.wait_recv()
    r_minus.wait_recv()
    r_far.wait_recv()
    r_sib = go(remote(rows.at[lo, :, core], rows.at[lo, :, core], R_SIB, sib))
    c_partner.wait_recv()
    c_pplus = go(ccopy(qh, C_PPLUS, yp))
    c_pminus = go(ccopy(qh, C_PMINUS, ym))

    c_pfar = ccopy(rf, C_PFAR, hip)
    r_psib = remote(rows.at[1 - lo, :, core], rows.at[1 - lo, :, core], R_PSIB, sib)

    grand = small[0]
    for d in range(1, 8):
        totals[d - 1].wait_recv()
        grand = grand + small_in[d]
    log_total = jnp.log(grand[0:1, 0:1])

    def turn_rows(l):
        for zz in range(4):
            for k in range(2):
                at = pl.ds(pl.multiple_of(l * 1024 + (zz * 2 + k) * 128, 128), 128)
                rowsT[:, at] = jnp.transpose(rows[l, zz, k].astype(F32)).astype(BF16)

    r_sib.wait_recv()
    turn_rows(lo)

    def piece(conf, score, base):
        x = score - base
        t = conf * x
        g = jnp.exp2(jnp.where(conf > 0, -1e4, x) * LOG2E)
        d = g + 2.0 ** -SHIFT
        slope = (t + g * pltpu.reciprocal(d, approx=True)).astype(BF16)
        fold = (PIECE // 8, 8, 256)
        return slope, jnp.sum((t * x).reshape(fold), axis=0), jnp.sum(jnp.log2(d).reshape(fold), axis=0)

    def kind_of(u):
        return jnp.where((u == 0) | (u == 3), CROSS, jnp.where((u == 1) | (u == 2), FAR, jnp.where(u <= 6, u - 4, 5 + (u - 7) // 2)))

    def plane_of(u):
        return jnp.where((u <= 1) | ((u >= 8) & (u % 2 == 0)), lo, 1 - lo)

    def block_of(kind):
        off = jnp.where((kind == NEXT) | (kind == CROSS_NEXT), 1, jnp.where(
            (kind == LAST) | (kind == CROSS_LAST), 3, jnp.where((kind == FAR) | (kind == CROSS_FAR), 2, 0)))
        h = jnp.where((kind <= LAST) | (kind == FAR), hi, 1 - hi)
        return h * 4 + (y + off) % 4

    def row_base(l, q):
        return pl.multiple_of(l * 1024 + q * TILE, TILE)

    def do_scores(dst, l, q, blk):
        tile = rows[l, 2 * q:2 * q + 2].reshape(TILE, K)
        dst[...] = lax.dot_general(
            tile, cols[blk], (((1,), (1,)), ((), ())), preferred_element_type=F32) - log_total

    def elementwise(src, dst, l, q, c0):
        la = jnp.zeros((8, 256), F32)
        lb = jnp.zeros((8, 256), F32)
        for v in range(TILE // PIECE):
            at = slice(v * PIECE, (v + 1) * PIECE)
            ra = pl.ds(pl.multiple_of(l * 1024 + q * TILE + v * PIECE, PIECE), PIECE)
            dst[at], a, b = piece(C[ra, pl.ds(c0, 256)], src[at], B[ra, pl.ds(c0, 256)])
            la = la + a
            lb = lb + b
        lacc[...] += la * 0.5 + (lb + float(SHIFT * TILE // 8)) * LN2

    def gradients(src, l, q, blk, kind):
        at = pl.ds(row_base(l, q), TILE)
        rg[at, :] += jnp.dot(src[...], cols[blk], preferred_element_type=F32)
        cg[kind] += jnp.dot(rowsT[:, at], src[...], preferred_element_type=F32)

    S_FAR, S_NEXT_RELAY, S_LAST_RELAY, S_CROSS_FAR, S_CROSS, S_NEXT, S_LAST = range(7)
    col_dest = [rf, row_at(hi, y + 1), row_at(hi, y - 1), row_at(1 - hi, y + 2), qh, row_at(hi, y + 1), row_at(hi, y - 1)]

    def col_copy(j):
        return remote(csend.at[j], cpart.at[j], G_COLS + j, (col_dest[j], c))

    def send_cols(j, value):
        csend[j] = value.astype(BF16)
        col_copy(j).start()

    OFFS = (2, 1, 3, 0)

    def rg_block(l, off, k):
        p = l * 4 + (z + off) % 4
        return rg[pl.ds(pl.multiple_of((p * 2 + k) * 128, 128), 128), :]

    sib_batch = remote(rsend.at[0:4], rsib.at[0:4], G_SIB, sib)

    def sib_copy(i):
        return remote(rsend.at[i], rsib.at[i], G_SIB + i, sib)

    def row_copy(i):
        dev = lop if i == 3 else (r, col_at(lo, z + OFFS[i % 4], core))
        return remote(rsum.at[i], rpart.at[i], G_ROWS + i, dev)

    def send_rows(i, value):
        rsum[i] = value.astype(BF16)
        row_copy(i).start()

    def at_step(u):
        return plane_of(u), block_of(kind_of(u)), kind_of(u)

    def tile_scores(dst, u, q):
        l, blk, _ = at_step(u)
        do_scores(dst, l, q, blk)

    def tile_slopes(src, dst, u, q):
        l, blk, _ = at_step(u)
        elementwise(src, dst, l, q, pl.multiple_of(blk * 256, 256))

    def tile_gradients(src, u, q):
        l, blk, kind = at_step(u)
        gradients(src, l, q, blk, kind)

    c_far.wait_recv()
    c_pfar.start()
    r_pplus.wait_recv()
    r_pminus.wait_recv()
    r_pfar.wait_recv()
    r_psib.start()
    tile_scores(scores_a, 0, 0)
    tile_scores(scores_b, 0, 1)
    tile_slopes(scores_a, slopes_a, 0, 0)
    tile_scores(scores_a, 1, 0)
    tile_slopes(scores_b, slopes_b, 0, 1)
    tile_gradients(slopes_a, 0, 0)
    tile_scores(scores_b, 1, 1)
    tile_slopes(scores_a, slopes_a, 1, 0)
    tile_gradients(slopes_b, 0, 1)
    tile_slopes(scores_b, slopes_b, 1, 1)
    tile_gradients(slopes_a, 1, 0)
    r_psib.wait_recv()
    c_plus.wait_recv()
    c_minus.wait_recv()
    turn_rows(1 - lo)
    tile_scores(scores_a, 2, 0)

    def steps(m, carry):
        u = m * 2

        @pl.when(m == 2)
        def _():
            send_cols(S_FAR, cg[FAR])

        @pl.when(m == 3)
        def _():
            c_pminus.wait_recv()

        @pl.when(m == 4)
        def _():
            c_pplus.wait_recv()

        @pl.when(m == 5)
        def _():
            send_cols(S_NEXT_RELAY, cg[CROSS_NEXT])
            c_pfar.wait_recv()

        tile_scores(scores_b, u, 1)
        tile_slopes(scores_a, slopes_a, u, 0)
        tile_gradients(slopes_b, u - 1, 1)
        tile_scores(scores_a, u + 1, 0)
        tile_slopes(scores_b, slopes_b, u, 1)
        tile_gradients(slopes_a, u, 0)
        tile_scores(scores_b, u + 1, 1)
        tile_slopes(scores_a, slopes_a, u + 1, 0)
        tile_gradients(slopes_b, u, 1)
        tile_scores(scores_a, u + 2, 0)
        tile_slopes(scores_b, slopes_b, u + 1, 1)
        tile_gradients(slopes_a, u + 1, 0)
        return carry

    lax.fori_loop(1, 6, steps, 0)

    send_cols(S_LAST_RELAY, cg[CROSS_LAST])
    tile_scores(scores_b, 12, 1)
    tile_slopes(scores_a, slopes_a, 12, 0)
    tile_gradients(slopes_b, 11, 1)
    for i in range(4):
        rsend[i] = rg_block(1 - lo, OFFS[i], 1 - core).astype(BF16)
    sib_batch.start()
    tile_slopes(scores_b, slopes_b, 12, 1)
    tile_gradients(slopes_a, 12, 0)

    qcols = [r, row_at(hi, y + 1), row_at(hi, y - 1)]
    for h in range(3):
        colsq[h * 256:(h + 1) * 256] = cols[qcols[h]]
        cgq[:, h * 256:(h + 1) * 256] = cg[h]

    def chip_of(t):
        off = jnp.where(t == 0, 2, jnp.where(t == 1, 1, jnp.where(t == 2, 3, 0)))
        return (z + off) % 4

    def q_rows(t, v, size):
        return pl.ds(pl.multiple_of(lo * 1024 + chip_of(t) * 256 + v, size), size)

    def q_scores(dst, t):
        tile = rows[lo, chip_of(t)].reshape(256, K)
        dst[...] = lax.dot_general(
            tile, colsq[...], (((1,), (1,)), ((), ())), preferred_element_type=F32) - log_total

    def q_elementwise(src, dst, t):
        la = jnp.zeros((8, 256), F32)
        lb = jnp.zeros((8, 256), F32)
        for h in range(3):
            c0 = pl.multiple_of(qcols[h] * 256, 256)
            for v in range(256 // PIECE):
                at = slice(v * PIECE, (v + 1) * PIECE)
                to = slice(h * 256, (h + 1) * 256)
                ra = q_rows(t, v * PIECE, PIECE)
                dst[at, to], a, b = piece(C[ra, pl.ds(c0, 256)], src[at, to], B[ra, pl.ds(c0, 256)])
                la = la + a
                lb = lb + b
        lacc[...] += la * 0.5 + (lb + float(SHIFT * WIDTH // 8)) * LN2

    def q_gradients(src, t):
        at = q_rows(t, 0, 256)
        rg[at, :] += jnp.dot(src[...], colsq[...], preferred_element_type=F32)
        cgq[...] += jnp.dot(rowsT[:, at], src[...], preferred_element_type=F32)

    def to_sibling(t):
        rsend[4 + t] = rg_block(lo, OFFS[t], 1 - core).astype(BF16)
        sib_copy(4 + t).start()

    def to_owner(t):
        sib_copy(4 + t).wait_recv()
        send_rows(4 + t, rg_block(lo, OFFS[t], core) + rsib[4 + t].astype(F32))

    tile_gradients(slopes_b, 12, 1)
    q_scores(sq_a, 0)
    send_cols(S_CROSS_FAR, cg[CROSS_FAR])
    sib_batch.wait_recv()
    for i in range(3):
        send_rows(i, rg_block(1 - lo, OFFS[i], core) + rsib[i].astype(F32))

    q_scores(sq_b, 1)
    q_elementwise(sq_a, tq_a, 0)
    q_scores(sq_a, 2)
    q_elementwise(sq_b, tq_b, 1)
    q_gradients(tq_a, 0)
    to_sibling(0)
    q_scores(sq_b, 3)
    q_elementwise(sq_a, tq_a, 2)
    q_gradients(tq_b, 1)
    to_sibling(1)
    to_owner(0)
    q_elementwise(sq_b, tq_b, 3)
    q_gradients(tq_a, 2)
    to_sibling(2)
    to_owner(1)
    small[1] = jnp.broadcast_to(
        jnp.sum(jnp.sum(lacc[...], axis=0, keepdims=True), axis=1, keepdims=True), (8, 128))
    losses = []
    for d in range(1, 8):
        losses.append(small_copy(small.at[1], small_row.at[d], 7 + d, ((r + d) % 8, c)))
        losses[-1].start()
    q_gradients(tq_b, 3)
    send_cols(S_NEXT, cgq[:, 256:512])
    send_cols(S_LAST, cgq[:, 512:768])
    to_sibling(3)
    to_owner(2)

    col_copy(S_NEXT_RELAY).wait_recv()
    col_copy(S_LAST_RELAY).wait_recv()
    send_cols(S_CROSS, cg[CROSS] + cpart[S_NEXT_RELAY].astype(F32) + cpart[S_LAST_RELAY].astype(F32))
    grad = rg_block(1 - lo, 0, core) + rsib[3].astype(F32)
    for i in range(3):
        row_copy(i).wait_recv()
        grad = grad + rpart[i].astype(F32)
    send_rows(3, grad)

    loss = small[1]
    for d in range(1, 8):
        losses[d - 1].wait_recv()
        loss = loss + small_row[d]
    small[2] = loss
    for d in range(1, 16):
        losses.append(small_copy(small.at[2], small_col.at[d], 14 + d, (r, (c + d) % 16)))
        losses[-1].start()

    sib_copy(7).wait_recv()
    grad = rg_block(lo, 0, core) + rsib[7].astype(F32)
    for i in range(4, 7):
        row_copy(i).wait_recv()
        grad = grad + rpart[i].astype(F32)
    total = cgq[:, 0:256]
    for j in (S_FAR, S_NEXT, S_LAST, S_CROSS_FAR, S_CROSS):
        col_copy(j).wait_recv()
        total = total + cpart[j].astype(F32)
    column_grad[...] = jnp.transpose(total)
    row_copy(3).wait_recv()
    row_grad[...] = grad + rpart[3].astype(F32)

    loss = small[2]
    for d in range(1, 16):
        losses[6 + d].wait_recv()
        loss = loss + small_col[d]
    mean_loss[...] = loss * (1.0 / 536870912.0)

    for copy in sent + totals + losses + [c_pfar, r_psib, sib_batch]:
        copy.wait_send()
    for j in range(7):
        col_copy(j).wait_send()
    for i in range(4, 8):
        sib_copy(i).wait_send()
    for i in range(7):
        row_copy(i).wait_send()


def update(
    row_grad, column_grad, loss, row_vectors, column_vectors, row_squares, column_squares,
    new_rows, new_columns, squares_row, squares_column, mean_loss,
):
    g = row_grad[...]
    s = row_squares[...] + g * g
    squares_row[...] = s
    new_rows[...] = row_vectors[...] - g * lax.rsqrt(s)
    g = column_grad[...]
    s = column_squares[...] + g * g
    squares_column[...] = s
    new_columns[...] = column_vectors[...] - g * lax.rsqrt(s)
    mean_loss[0, 0] = loss[0, 0]


def on_device(
    counts, row_totals, column_totals, row_vectors, column_vectors, row_squares, column_squares
):
    vmem = pl.BlockSpec(memory_space=pltpu.VMEM)
    smem = pl.BlockSpec(memory_space=pltpu.SMEM)
    row_grad, column_grad, loss = pl.pallas_call(
        kernel,
        out_shape=[
            jax.ShapeDtypeStruct((128, K), F32),
            jax.ShapeDtypeStruct((256, K), F32),
            jax.ShapeDtypeStruct((8, 128), F32),
        ],
        in_specs=[pl.BlockSpec(memory_space=pl.ANY)] + [vmem] * 4,
        out_specs=[vmem] * 3,
        scratch_shapes=[
            pltpu.VMEM((SLOTS, STRIP, NC), jnp.int32),
            pltpu.VMEM((NR, 128), F32),
            pltpu.VMEM((8, NC), F32),
            pltpu.VMEM((NR, NC), F32),
            pltpu.VMEM((NR, NC), F32),
            pltpu.VMEM((2, 4, 2, 128, K), BF16),
            pltpu.VMEM((K, NR), BF16),
            pltpu.VMEM((8, 256, K), BF16),
            pltpu.VMEM((WIDTH, K), BF16),
            pltpu.VMEM((NR, K), F32),
            pltpu.VMEM((8, K, 256), F32),
            pltpu.VMEM((K, WIDTH), F32),
            pltpu.VMEM((TILE, 256), BF16),
            pltpu.VMEM((TILE, 256), BF16),
            pltpu.VMEM((TILE, 256), F32),
            pltpu.VMEM((TILE, 256), F32),
            pltpu.VMEM((256, WIDTH), F32),
            pltpu.VMEM((256, WIDTH), F32),
            pltpu.VMEM((256, WIDTH), BF16),
            pltpu.VMEM((256, WIDTH), BF16),
            pltpu.VMEM((8, 256), F32),
            pltpu.VMEM((7, K, 256), BF16),
            pltpu.VMEM((7, K, 256), BF16),
            pltpu.VMEM((8, 128, K), BF16),
            pltpu.VMEM((8, 128, K), BF16),
            pltpu.VMEM((8, 128, K), BF16),
            pltpu.VMEM((8, 128, K), BF16),
            pltpu.VMEM((3, 8, 128), F32),
            pltpu.VMEM((8, 8, 128), F32),
            pltpu.VMEM((8, 8, 128), F32),
            pltpu.VMEM((16, 8, 128), F32),
            pltpu.SemaphoreType.DMA((SLOTS,)),
            pltpu.SemaphoreType.DMA((N_SEMS,)),
            pltpu.SemaphoreType.DMA((N_SEMS,)),
            pltpu.SemaphoreType.DMA((32,)),
            pltpu.SemaphoreType.DMA((32,)),
        ],
        compiler_params=pltpu.CompilerParams(
            collective_id=0, has_side_effects=True, vmem_limit_bytes=63 * 1024 * 1024),
        name="swivel_step",
    )(counts, row_totals.reshape(16, 128), column_totals.reshape(1, NC), row_vectors, column_vectors)
    outs = pl.pallas_call(
        update,
        out_shape=[
            jax.ShapeDtypeStruct((128, K), F32),
            jax.ShapeDtypeStruct((256, K), F32),
            jax.ShapeDtypeStruct((128, K), F32),
            jax.ShapeDtypeStruct((256, K), F32),
            jax.ShapeDtypeStruct((1, 1), F32),
        ],
        in_specs=[vmem, vmem, smem] + [vmem] * 4,
        out_specs=[vmem] * 4 + [smem],
        name="adagrad_update",
    )(row_grad, column_grad, loss, row_vectors, column_vectors, row_squares, column_squares)
    return outs[0], outs[1], outs[2], outs[3], outs[4].reshape(())


def solution(mesh):
    in_specs = (
        P("row", "col"),
        P("row"),
        P("col"),
        P(("row", "col"), None),
        P(("col", "row"), None),
        P(("row", "col"), None),
        P(("col", "row"), None),
    )
    out_specs = (
        P(("row", "col"), None),
        P(("col", "row"), None),
        P(("row", "col"), None),
        P(("col", "row"), None),
        P(),
    )
    return jax.shard_map(
        on_device, mesh=mesh, in_specs=in_specs, out_specs=out_specs, check_vma=False
    )
```

```python
import jax
import jax.numpy as jnp
from jax import lax
from jax.experimental import pallas as pl
from jax.experimental.pallas import tpu as pltpu
from jax.sharding import PartitionSpec as P

F32 = jnp.float32
BF16 = jnp.bfloat16
LOG2E = 1.4426950408889634
LN2 = 0.6931471805599453
SHIFT = 20
K = 256
NR = 2048
NC = 2048
STRIP = 128
SLOTS = 6
TILE = 512
PIECE = 16

R_PARTNER, R_PLUS, R_MINUS, R_FAR, R_PPLUS, R_PMINUS, R_PFAR, R_SPARE, R_SIB, R_PSIB = range(10)
C_PARTNER, C_PLUS, C_MINUS, C_FAR, C_PPLUS, C_PMINUS, C_PFAR = range(10, 17)
G_COLS = 17
G_SIB = 24
G_ROWS = 32
N_SEMS = 40
WIDTH = 768
OWN, NEXT, LAST, CROSS, FAR, CROSS_NEXT, CROSS_LAST, CROSS_FAR = range(8)


def kernel(
    counts, row_totals, column_totals, row_vectors, column_vectors,
    row_grad, column_grad, mean_loss,
    cbuf, lrow, lcol, B, C, rows, rowsT, cols, colsq, rg, cg, cgq, slopes_a, slopes_b, scores_a, scores_b,
    sq_a, sq_b, tq_a, tq_b, lacc,
    csend, cpart, rsend, rsib, rsum, rpart, small, small_in, small_row, small_col,
    csem, ssem, rsem, small_s, small_r,
):
    r = lax.axis_index("row")
    c = lax.axis_index("col")
    hi, y = r // 4, r % 4
    lo, z, core = c // 8, (c // 2) % 4, c % 2

    def row_at(h, yy):
        return h * 4 + (yy + 4) % 4

    def col_at(l, zz, k):
        return l * 8 + ((zz + 4) % 4) * 2 + k

    def remote(src, dst, which, dev):
        return pltpu.make_async_remote_copy(
            src_ref=src, dst_ref=dst, send_sem=ssem.at[which], recv_sem=rsem.at[which],
            device_id=dev, device_id_type=pl.DeviceIdType.MESH)

    def small_copy(src, dst, which, dev):
        return pltpu.make_async_remote_copy(
            src_ref=src, dst_ref=dst, send_sem=small_s.at[which], recv_sem=small_r.at[which],
            device_id=dev, device_id_type=pl.DeviceIdType.MESH)

    def strip(i, slot):
        return pltpu.make_async_copy(
            counts.at[pl.ds(pl.multiple_of(i * STRIP, STRIP), STRIP)], cbuf.at[slot], csem.at[slot])

    for s in range(SLOTS):
        strip(s, s).start()

    barrier = pltpu.get_barrier_semaphore()
    for d in range(1, 8):
        pl.semaphore_signal(barrier, inc=1, device_id=((r + d) % 8, c), device_id_type=pl.DeviceIdType.MESH)
    for d in range(1, 16):
        pl.semaphore_signal(barrier, inc=1, device_id=(r, (c + d) % 16), device_id_type=pl.DeviceIdType.MESH)

    rows[lo, z, core] = row_vectors[...].astype(BF16)
    cols[r] = column_vectors[...].astype(BF16)
    part = jnp.sum(row_totals[...].astype(F32), axis=0, keepdims=True)
    small[0] = jnp.broadcast_to(jnp.sum(part, axis=1, keepdims=True), (8, 128))
    for b in range(16):
        v = jnp.log(row_totals[b:b + 1, :].astype(F32))
        lrow[b * 128:(b + 1) * 128, :] = jnp.transpose(jnp.broadcast_to(v, (128, 128)))
    lcol[...] = jnp.broadcast_to(jnp.log(column_totals[...].astype(F32)), (8, NC))

    def prepare(first, last):
        def one(i, carry):
            slot = i % SLOTS
            strip(i, slot).wait()

            def inner(t, carry):
                t8 = pl.multiple_of(t * 8, 8)
                r0 = pl.multiple_of(i * STRIP + t * 8, 8)
                lr = lrow[pl.ds(r0, 8), :]
                for q in range(NC // 128):
                    at = slice(q * 128, (q + 1) * 128)
                    n = cbuf[slot, pl.ds(t8, 8), at].astype(F32)
                    m = jnp.maximum(n, 1.0)
                    seen = n > 0
                    B[pl.ds(r0, 8), at] = jnp.where(seen, jnp.log(m), SHIFT * LN2) - lr - lcol[:, at]
                    C[pl.ds(r0, 8), at] = jnp.where(seen, (0.25 * n) * lax.rsqrt(m) + 0.1, 0.0)
                return carry

            lax.fori_loop(0, STRIP // 8, inner, 0, unroll=8)

            @pl.when(i + SLOTS < NR // STRIP)
            def _():
                strip(i + SLOTS, slot).start()

            return carry

        lax.fori_loop(first, last, one, 0)

    prepare(0, 3)
    pl.semaphore_wait(barrier, 22)

    zp, zm, zz2 = (r, col_at(lo, z + 1, core)), (r, col_at(lo, z - 1, core)), (r, col_at(lo, z + 2, core))
    lop = (r, col_at(1 - lo, z, core))
    sib = (r, col_at(lo, z, 1 - core))
    yp, ym, yy2 = (row_at(hi, y + 1), c), (row_at(hi, y - 1), c), (row_at(hi, y + 2), c)
    hip = (row_at(1 - hi, y), c)
    rf = row_at(hi, y + 2)
    qh = row_at(1 - hi, y)

    def rcopy(l, zz, which, dev):
        return remote(rows.at[l, zz, core], rows.at[l, zz, core], which, dev)

    def ccopy(q, which, dev):
        return remote(cols.at[q], cols.at[q], which, dev)

    sent = []

    def go(copy):
        copy.start()
        sent.append(copy)
        return copy

    r_partner = go(rcopy(lo, z, R_PARTNER, lop))
    r_plus = go(rcopy(lo, z, R_PLUS, zp))
    r_minus = go(rcopy(lo, z, R_MINUS, zm))
    r_far = go(rcopy(lo, z, R_FAR, zz2))
    c_partner = go(ccopy(r, C_PARTNER, hip))
    c_plus = go(ccopy(r, C_PLUS, yp))
    c_minus = go(ccopy(r, C_MINUS, ym))
    c_far = go(ccopy(r, C_FAR, yy2))
    totals = []
    for d in range(1, 8):
        totals.append(small_copy(small.at[0], small_in.at[d], d, ((r + d) % 8, c)))
        totals[-1].start()

    prepare(3, 11)
    rg[...] = jnp.zeros_like(rg)
    lacc[...] = jnp.zeros_like(lacc)
    slopes_b[...] = jnp.zeros_like(slopes_b)
    cg[...] = jnp.zeros_like(cg)

    r_partner.wait_recv()
    r_pplus = go(rcopy(1 - lo, z, R_PPLUS, zp))
    r_pminus = go(rcopy(1 - lo, z, R_PMINUS, zm))
    r_pfar = go(rcopy(1 - lo, z, R_PFAR, zz2))
    prepare(11, 14)
    r_plus.wait_recv()
    r_minus.wait_recv()
    r_far.wait_recv()
    r_sib = go(remote(rows.at[lo, :, core], rows.at[lo, :, core], R_SIB, sib))
    prepare(14, 16)
    c_partner.wait_recv()
    c_pplus = go(ccopy(qh, C_PPLUS, yp))
    c_pminus = go(ccopy(qh, C_PMINUS, ym))

    c_pfar = ccopy(rf, C_PFAR, hip)
    r_psib = remote(rows.at[1 - lo, :, core], rows.at[1 - lo, :, core], R_PSIB, sib)

    grand = small[0]
    for d in range(1, 8):
        totals[d - 1].wait_recv()
        grand = grand + small_in[d]
    log_total = jnp.log(grand[0:1, 0:1])

    def turn_rows(l):
        for zz in range(4):
            for k in range(2):
                at = pl.ds(pl.multiple_of(l * 1024 + (zz * 2 + k) * 128, 128), 128)
                rowsT[:, at] = jnp.transpose(rows[l, zz, k].astype(F32)).astype(BF16)

    r_sib.wait_recv()
    turn_rows(lo)

    def piece(conf, score, base):
        x = score - base
        t = conf * x
        g = jnp.exp2(jnp.where(conf > 0, -1e4, x) * LOG2E)
        d = g + 2.0 ** -SHIFT
        slope = (t + g * pltpu.reciprocal(d, approx=True)).astype(BF16)
        fold = (PIECE // 8, 8, 256)
        return slope, jnp.sum((t * x).reshape(fold), axis=0), jnp.sum(jnp.log2(d).reshape(fold), axis=0)

    def kind_of(u):
        return jnp.where((u == 0) | (u == 3), CROSS, jnp.where((u == 1) | (u == 2), FAR, jnp.where(u <= 6, u - 4, 5 + (u - 7) // 2)))

    def plane_of(u):
        return jnp.where((u <= 1) | ((u >= 8) & (u % 2 == 0)), lo, 1 - lo)

    def block_of(kind):
        off = jnp.where((kind == NEXT) | (kind == CROSS_NEXT), 1, jnp.where(
            (kind == LAST) | (kind == CROSS_LAST), 3, jnp.where((kind == FAR) | (kind == CROSS_FAR), 2, 0)))
        h = jnp.where((kind <= LAST) | (kind == FAR), hi, 1 - hi)
        return h * 4 + (y + off) % 4

    def row_base(l, q):
        return pl.multiple_of(l * 1024 + q * TILE, TILE)

    def do_scores(dst, l, q, blk):
        tile = rows[l, 2 * q:2 * q + 2].reshape(TILE, K)
        dst[...] = lax.dot_general(
            tile, cols[blk], (((1,), (1,)), ((), ())), preferred_element_type=F32) - log_total

    def elementwise(src, dst, l, q, c0):
        la = jnp.zeros((8, 256), F32)
        lb = jnp.zeros((8, 256), F32)
        for v in range(TILE // PIECE):
            at = slice(v * PIECE, (v + 1) * PIECE)
            ra = pl.ds(pl.multiple_of(l * 1024 + q * TILE + v * PIECE, PIECE), PIECE)
            dst[at], a, b = piece(C[ra, pl.ds(c0, 256)], src[at], B[ra, pl.ds(c0, 256)])
            la = la + a
            lb = lb + b
        lacc[...] += la * 0.5 + (lb + float(SHIFT * TILE // 8)) * LN2

    def gradients(src, l, q, blk, kind):
        at = pl.ds(row_base(l, q), TILE)
        rg[at, :] += jnp.dot(src[...], cols[blk], preferred_element_type=F32)
        cg[kind] += jnp.dot(rowsT[:, at], src[...], preferred_element_type=F32)

    S_FAR, S_NEXT_RELAY, S_LAST_RELAY, S_CROSS_FAR, S_CROSS, S_NEXT, S_LAST = range(7)
    col_dest = [rf, row_at(hi, y + 1), row_at(hi, y - 1), row_at(1 - hi, y + 2), qh, row_at(hi, y + 1), row_at(hi, y - 1)]

    def col_copy(j):
        return remote(csend.at[j], cpart.at[j], G_COLS + j, (col_dest[j], c))

    def send_cols(j, value):
        csend[j] = value.astype(BF16)
        col_copy(j).start()

    OFFS = (2, 1, 3, 0)

    def rg_block(l, off, k):
        p = l * 4 + (z + off) % 4
        return rg[pl.ds(pl.multiple_of((p * 2 + k) * 128, 128), 128), :]

    sib_batch = remote(rsend.at[0:4], rsib.at[0:4], G_SIB, sib)

    def sib_copy(i):
        return remote(rsend.at[i], rsib.at[i], G_SIB + i, sib)

    def row_copy(i):
        dev = lop if i == 3 else (r, col_at(lo, z + OFFS[i % 4], core))
        return remote(rsum.at[i], rpart.at[i], G_ROWS + i, dev)

    def send_rows(i, value):
        rsum[i] = value.astype(BF16)
        row_copy(i).start()

    def at_step(u):
        return plane_of(u), block_of(kind_of(u)), kind_of(u)

    def tile_scores(dst, u, q):
        l, blk, _ = at_step(u)
        do_scores(dst, l, q, blk)

    def tile_slopes(src, dst, u, q):
        l, blk, _ = at_step(u)
        elementwise(src, dst, l, q, pl.multiple_of(blk * 256, 256))

    def tile_gradients(src, u, q):
        l, blk, kind = at_step(u)
        gradients(src, l, q, blk, kind)

    c_far.wait_recv()
    c_pfar.start()
    r_pplus.wait_recv()
    r_pminus.wait_recv()
    r_pfar.wait_recv()
    r_psib.start()
    tile_scores(scores_a, 0, 0)
    tile_scores(scores_b, 0, 1)
    tile_slopes(scores_a, slopes_a, 0, 0)
    tile_scores(scores_a, 1, 0)
    tile_slopes(scores_b, slopes_b, 0, 1)
    tile_gradients(slopes_a, 0, 0)
    tile_scores(scores_b, 1, 1)
    tile_slopes(scores_a, slopes_a, 1, 0)
    tile_gradients(slopes_b, 0, 1)
    tile_slopes(scores_b, slopes_b, 1, 1)
    tile_gradients(slopes_a, 1, 0)
    r_psib.wait_recv()
    c_plus.wait_recv()
    c_minus.wait_recv()
    turn_rows(1 - lo)
    tile_scores(scores_a, 2, 0)

    def run_if(test):
        return (lambda body: body()) if test else (lambda body: None)

    def steps(m, carry):
        u = m * 2

        @run_if(m == 2)
        def _():
            send_cols(S_FAR, cg[FAR])

        @run_if(m == 3)
        def _():
            c_pminus.wait_recv()

        @run_if(m == 4)
        def _():
            c_pplus.wait_recv()

        @run_if(m == 5)
        def _():
            send_cols(S_NEXT_RELAY, cg[CROSS_NEXT])
            c_pfar.wait_recv()

        tile_scores(scores_b, u, 1)
        tile_slopes(scores_a, slopes_a, u, 0)
        tile_gradients(slopes_b, u - 1, 1)
        tile_scores(scores_a, u + 1, 0)
        tile_slopes(scores_b, slopes_b, u, 1)
        tile_gradients(slopes_a, u, 0)
        tile_scores(scores_b, u + 1, 1)
        tile_slopes(scores_a, slopes_a, u + 1, 0)
        tile_gradients(slopes_b, u, 1)
        tile_scores(scores_a, u + 2, 0)
        tile_slopes(scores_b, slopes_b, u + 1, 1)
        tile_gradients(slopes_a, u + 1, 0)
        return carry

    for m in range(1, 6):
        steps(m, 0)

    send_cols(S_LAST_RELAY, cg[CROSS_LAST])
    tile_scores(scores_b, 12, 1)
    tile_slopes(scores_a, slopes_a, 12, 0)
    tile_gradients(slopes_b, 11, 1)
    for i in range(4):
        rsend[i] = rg_block(1 - lo, OFFS[i], 1 - core).astype(BF16)
    sib_batch.start()
    tile_slopes(scores_b, slopes_b, 12, 1)
    tile_gradients(slopes_a, 12, 0)

    qcols = [r, row_at(hi, y + 1), row_at(hi, y - 1)]
    for h in range(3):
        colsq[h * 256:(h + 1) * 256] = cols[qcols[h]]
        cgq[:, h * 256:(h + 1) * 256] = cg[h]

    def chip_of(t):
        off = jnp.where(t == 0, 2, jnp.where(t == 1, 1, jnp.where(t == 2, 3, 0)))
        return (z + off) % 4

    def q_rows(t, v, size):
        return pl.ds(pl.multiple_of(lo * 1024 + chip_of(t) * 256 + v, size), size)

    def q_scores(dst, t):
        tile = rows[lo, chip_of(t)].reshape(256, K)
        dst[...] = lax.dot_general(
            tile, colsq[...], (((1,), (1,)), ((), ())), preferred_element_type=F32) - log_total

    def q_elementwise(src, dst, t):
        la = jnp.zeros((8, 256), F32)
        lb = jnp.zeros((8, 256), F32)
        for h in range(3):
            c0 = pl.multiple_of(qcols[h] * 256, 256)
            for v in range(256 // PIECE):
                at = slice(v * PIECE, (v + 1) * PIECE)
                to = slice(h * 256, (h + 1) * 256)
                ra = q_rows(t, v * PIECE, PIECE)
                dst[at, to], a, b = piece(C[ra, pl.ds(c0, 256)], src[at, to], B[ra, pl.ds(c0, 256)])
                la = la + a
                lb = lb + b
        lacc[...] += la * 0.5 + (lb + float(SHIFT * WIDTH // 8)) * LN2

    def q_gradients(src, t):
        at = q_rows(t, 0, 256)
        rg[at, :] += jnp.dot(src[...], colsq[...], preferred_element_type=F32)
        cgq[...] += jnp.dot(rowsT[:, at], src[...], preferred_element_type=F32)

    def to_sibling(t):
        rsend[4 + t] = rg_block(lo, OFFS[t], 1 - core).astype(BF16)
        sib_copy(4 + t).start()

    def to_owner(t):
        sib_copy(4 + t).wait_recv()
        send_rows(4 + t, rg_block(lo, OFFS[t], core) + rsib[4 + t].astype(F32))

    tile_gradients(slopes_b, 12, 1)
    q_scores(sq_a, 0)
    send_cols(S_CROSS_FAR, cg[CROSS_FAR])
    sib_batch.wait_recv()
    for i in range(3):
        send_rows(i, rg_block(1 - lo, OFFS[i], core) + rsib[i].astype(F32))

    q_scores(sq_b, 1)
    q_elementwise(sq_a, tq_a, 0)
    q_scores(sq_a, 2)
    q_elementwise(sq_b, tq_b, 1)
    q_gradients(tq_a, 0)
    to_sibling(0)
    q_scores(sq_b, 3)
    q_elementwise(sq_a, tq_a, 2)
    q_gradients(tq_b, 1)
    to_sibling(1)
    to_owner(0)
    q_elementwise(sq_b, tq_b, 3)
    q_gradients(tq_a, 2)
    to_sibling(2)
    to_owner(1)
    small[1] = jnp.broadcast_to(
        jnp.sum(jnp.sum(lacc[...], axis=0, keepdims=True), axis=1, keepdims=True), (8, 128))
    losses = []
    for d in range(1, 8):
        losses.append(small_copy(small.at[1], small_row.at[d], 7 + d, ((r + d) % 8, c)))
        losses[-1].start()
    q_gradients(tq_b, 3)
    send_cols(S_NEXT, cgq[:, 256:512])
    send_cols(S_LAST, cgq[:, 512:768])
    to_sibling(3)
    to_owner(2)

    col_copy(S_NEXT_RELAY).wait_recv()
    col_copy(S_LAST_RELAY).wait_recv()
    send_cols(S_CROSS, cg[CROSS] + cpart[S_NEXT_RELAY].astype(F32) + cpart[S_LAST_RELAY].astype(F32))
    grad = rg_block(1 - lo, 0, core) + rsib[3].astype(F32)
    for i in range(3):
        row_copy(i).wait_recv()
        grad = grad + rpart[i].astype(F32)
    send_rows(3, grad)

    loss = small[1]
    for d in range(1, 8):
        losses[d - 1].wait_recv()
        loss = loss + small_row[d]
    small[2] = loss
    for d in range(1, 16):
        losses.append(small_copy(small.at[2], small_col.at[d], 14 + d, (r, (c + d) % 16)))
        losses[-1].start()

    sib_copy(7).wait_recv()
    grad = rg_block(lo, 0, core) + rsib[7].astype(F32)
    for i in range(4, 7):
        row_copy(i).wait_recv()
        grad = grad + rpart[i].astype(F32)
    total = cgq[:, 0:256]
    for j in (S_FAR, S_NEXT, S_LAST, S_CROSS_FAR, S_CROSS):
        col_copy(j).wait_recv()
        total = total + cpart[j].astype(F32)
    column_grad[...] = jnp.transpose(total)
    row_copy(3).wait_recv()
    row_grad[...] = grad + rpart[3].astype(F32)

    loss = small[2]
    for d in range(1, 16):
        losses[6 + d].wait_recv()
        loss = loss + small_col[d]
    mean_loss[...] = loss * (1.0 / 536870912.0)

    for copy in sent + totals + losses + [c_pfar, r_psib, sib_batch]:
        copy.wait_send()
    for j in range(7):
        col_copy(j).wait_send()
    for i in range(4, 8):
        sib_copy(i).wait_send()
    for i in range(7):
        row_copy(i).wait_send()


def update(
    row_grad, column_grad, loss, row_vectors, column_vectors, row_squares, column_squares,
    new_rows, new_columns, squares_row, squares_column, mean_loss,
):
    g = row_grad[...]
    s = row_squares[...] + g * g
    squares_row[...] = s
    new_rows[...] = row_vectors[...] - g * lax.rsqrt(s)
    g = column_grad[...]
    s = column_squares[...] + g * g
    squares_column[...] = s
    new_columns[...] = column_vectors[...] - g * lax.rsqrt(s)
    mean_loss[0, 0] = loss[0, 0]


def on_device(
    counts, row_totals, column_totals, row_vectors, column_vectors, row_squares, column_squares
):
    vmem = pl.BlockSpec(memory_space=pltpu.VMEM)
    smem = pl.BlockSpec(memory_space=pltpu.SMEM)
    row_grad, column_grad, loss = pl.pallas_call(
        kernel,
        out_shape=[
            jax.ShapeDtypeStruct((128, K), F32),
            jax.ShapeDtypeStruct((256, K), F32),
            jax.ShapeDtypeStruct((8, 128), F32),
        ],
        in_specs=[pl.BlockSpec(memory_space=pl.ANY)] + [vmem] * 4,
        out_specs=[vmem] * 3,
        scratch_shapes=[
            pltpu.VMEM((SLOTS, STRIP, NC), jnp.int32),
            pltpu.VMEM((NR, 128), F32),
            pltpu.VMEM((8, NC), F32),
            pltpu.VMEM((NR, NC), F32),
            pltpu.VMEM((NR, NC), F32),
            pltpu.VMEM((2, 4, 2, 128, K), BF16),
            pltpu.VMEM((K, NR), BF16),
            pltpu.VMEM((8, 256, K), BF16),
            pltpu.VMEM((WIDTH, K), BF16),
            pltpu.VMEM((NR, K), F32),
            pltpu.VMEM((8, K, 256), F32),
            pltpu.VMEM((K, WIDTH), F32),
            pltpu.VMEM((TILE, 256), BF16),
            pltpu.VMEM((TILE, 256), BF16),
            pltpu.VMEM((TILE, 256), F32),
            pltpu.VMEM((TILE, 256), F32),
            pltpu.VMEM((256, WIDTH), F32),
            pltpu.VMEM((256, WIDTH), F32),
            pltpu.VMEM((256, WIDTH), BF16),
            pltpu.VMEM((256, WIDTH), BF16),
            pltpu.VMEM((8, 256), F32),
            pltpu.VMEM((7, K, 256), BF16),
            pltpu.VMEM((7, K, 256), BF16),
            pltpu.VMEM((8, 128, K), BF16),
            pltpu.VMEM((8, 128, K), BF16),
            pltpu.VMEM((8, 128, K), BF16),
            pltpu.VMEM((8, 128, K), BF16),
            pltpu.VMEM((3, 8, 128), F32),
            pltpu.VMEM((8, 8, 128), F32),
            pltpu.VMEM((8, 8, 128), F32),
            pltpu.VMEM((16, 8, 128), F32),
            pltpu.SemaphoreType.DMA((SLOTS,)),
            pltpu.SemaphoreType.DMA((N_SEMS,)),
            pltpu.SemaphoreType.DMA((N_SEMS,)),
            pltpu.SemaphoreType.DMA((32,)),
            pltpu.SemaphoreType.DMA((32,)),
        ],
        compiler_params=pltpu.CompilerParams(
            collective_id=0, has_side_effects=True, vmem_limit_bytes=63 * 1024 * 1024),
        name="swivel_step",
    )(counts, row_totals.reshape(16, 128), column_totals.reshape(1, NC), row_vectors, column_vectors)
    outs = pl.pallas_call(
        update,
        out_shape=[
            jax.ShapeDtypeStruct((128, K), F32),
            jax.ShapeDtypeStruct((256, K), F32),
            jax.ShapeDtypeStruct((128, K), F32),
            jax.ShapeDtypeStruct((256, K), F32),
            jax.ShapeDtypeStruct((1, 1), F32),
        ],
        in_specs=[vmem, vmem, smem] + [vmem] * 4,
        out_specs=[vmem] * 4 + [smem],
        name="adagrad_update",
    )(row_grad, column_grad, loss, row_vectors, column_vectors, row_squares, column_squares)
    return outs[0], outs[1], outs[2], outs[3], outs[4].reshape(())


def solution(mesh):
    in_specs = (
        P("row", "col"),
        P("row"),
        P("col"),
        P(("row", "col"), None),
        P(("col", "row"), None),
        P(("row", "col"), None),
        P(("col", "row"), None),
    )
    out_specs = (
        P(("row", "col"), None),
        P(("col", "row"), None),
        P(("row", "col"), None),
        P(("col", "row"), None),
        P(),
    )
    return jax.shard_map(
        on_device, mesh=mesh, in_specs=in_specs, out_specs=out_specs, check_vma=False
    )
```

```python
import jax
import jax.numpy as jnp
from jax import lax
from jax.experimental import pallas as pl
from jax.experimental.pallas import tpu as pltpu
from jax.sharding import PartitionSpec as P

F32 = jnp.float32
BF16 = jnp.bfloat16
LOG2E = 1.4426950408889634
LN2 = 0.6931471805599453
SHIFT = 20
K = 256
NR = 2048
NC = 2048
STRIP = 128
SLOTS = 6
TILE = 512
PIECE = 16

R_PARTNER, R_PLUS, R_MINUS, R_FAR, R_PPLUS, R_PMINUS, R_PFAR, R_SPARE, R_SIB, R_PSIB = range(10)
C_PARTNER, C_PLUS, C_MINUS, C_FAR, C_PPLUS, C_PMINUS, C_PFAR = range(10, 17)
G_COLS = 17
G_SIB = 24
G_ROWS = 32
N_SEMS = 40
WIDTH = 768
OWN, NEXT, LAST, CROSS, FAR, CROSS_NEXT, CROSS_LAST, CROSS_FAR = range(8)


def kernel(
    counts, row_totals_in, column_totals_in, row_vectors_in, column_vectors_in,
    row_grad, column_grad, mean_loss,
    row_totals, column_totals, row_vectors, column_vectors, cbuf, lrow, lcol, B, C, rows, rowsT, cols, colsq, rg, cg, cgq, slopes_a, slopes_b, scores_a, scores_b,
    sq_a, sq_b, tq_a, tq_b, lacc,
    csend, cpart, rsend, rsib, rsum, rpart, small, small_in, small_row, small_col,
    csem, isem, ssem, rsem, small_s, small_r,
):
    r = lax.axis_index("row")
    c = lax.axis_index("col")
    hi, y = r // 4, r % 4
    lo, z, core = c // 8, (c // 2) % 4, c % 2

    def row_at(h, yy):
        return h * 4 + (yy + 4) % 4

    def col_at(l, zz, k):
        return l * 8 + ((zz + 4) % 4) * 2 + k

    def remote(src, dst, which, dev):
        return pltpu.make_async_remote_copy(
            src_ref=src, dst_ref=dst, send_sem=ssem.at[which], recv_sem=rsem.at[which],
            device_id=dev, device_id_type=pl.DeviceIdType.MESH)

    def small_copy(src, dst, which, dev):
        return pltpu.make_async_remote_copy(
            src_ref=src, dst_ref=dst, send_sem=small_s.at[which], recv_sem=small_r.at[which],
            device_id=dev, device_id_type=pl.DeviceIdType.MESH)

    def strip(i, slot):
        return pltpu.make_async_copy(
            counts.at[pl.ds(pl.multiple_of(i * STRIP, STRIP), STRIP)], cbuf.at[slot], csem.at[slot])

    barrier = pltpu.get_barrier_semaphore()
    for d in range(1, 8):
        pl.semaphore_signal(barrier, inc=1, device_id=((r + d) % 8, c), device_id_type=pl.DeviceIdType.MESH)
    for d in range(1, 16):
        pl.semaphore_signal(barrier, inc=1, device_id=(r, (c + d) % 16), device_id_type=pl.DeviceIdType.MESH)
    inputs = [
        pltpu.make_async_copy(src, dst, isem.at[i]) for i, (src, dst) in enumerate((
            (row_totals_in, row_totals), (column_totals_in, column_totals),
            (row_vectors_in, row_vectors), (column_vectors_in, column_vectors)))]
    for copy in inputs:
        copy.start()
    for s in range(SLOTS):
        strip(s, s).start()
    for copy in inputs:
        copy.wait()

    rows[lo, z, core] = row_vectors[...].astype(BF16)
    cols[r] = column_vectors[...].astype(BF16)
    part = jnp.sum(row_totals[...].astype(F32), axis=0, keepdims=True)
    small[0] = jnp.broadcast_to(jnp.sum(part, axis=1, keepdims=True), (8, 128))
    for b in range(16):
        v = jnp.log(row_totals[b:b + 1, :].astype(F32))
        lrow[b * 128:(b + 1) * 128, :] = jnp.transpose(jnp.broadcast_to(v, (128, 128)))
    lcol[...] = jnp.broadcast_to(jnp.log(column_totals[...].astype(F32)), (8, NC))

    def prepare(first, last):
        def one(i, carry):
            slot = i % SLOTS
            strip(i, slot).wait()

            def inner(t, carry):
                t8 = pl.multiple_of(t * 8, 8)
                r0 = pl.multiple_of(i * STRIP + t * 8, 8)
                lr = lrow[pl.ds(r0, 8), :]
                for q in range(NC // 128):
                    at = slice(q * 128, (q + 1) * 128)
                    n = cbuf[slot, pl.ds(t8, 8), at].astype(F32)
                    m = jnp.maximum(n, 1.0)
                    seen = n > 0
                    B[pl.ds(r0, 8), at] = jnp.where(seen, jnp.log(m), SHIFT * LN2) - lr - lcol[:, at]
                    C[pl.ds(r0, 8), at] = jnp.where(seen, (0.25 * n) * lax.rsqrt(m) + 0.1, 0.0)
                return carry

            lax.fori_loop(0, STRIP // 8, inner, 0, unroll=8)

            @pl.when(i + SLOTS < NR // STRIP)
            def _():
                strip(i + SLOTS, slot).start()

            return carry

        lax.fori_loop(first, last, one, 0)

    prepare(0, 3)
    pl.semaphore_wait(barrier, 22)

    zp, zm, zz2 = (r, col_at(lo, z + 1, core)), (r, col_at(lo, z - 1, core)), (r, col_at(lo, z + 2, core))
    lop = (r, col_at(1 - lo, z, core))
    sib = (r, col_at(lo, z, 1 - core))
    yp, ym, yy2 = (row_at(hi, y + 1), c), (row_at(hi, y - 1), c), (row_at(hi, y + 2), c)
    hip = (row_at(1 - hi, y), c)
    rf = row_at(hi, y + 2)
    qh = row_at(1 - hi, y)

    def rcopy(l, zz, which, dev):
        return remote(rows.at[l, zz, core], rows.at[l, zz, core], which, dev)

    def ccopy(q, which, dev):
        return remote(cols.at[q], cols.at[q], which, dev)

    sent = []

    def go(copy):
        copy.start()
        sent.append(copy)
        return copy

    r_partner = go(rcopy(lo, z, R_PARTNER, lop))
    r_plus = go(rcopy(lo, z, R_PLUS, zp))
    r_minus = go(rcopy(lo, z, R_MINUS, zm))
    r_far = go(rcopy(lo, z, R_FAR, zz2))
    c_partner = go(ccopy(r, C_PARTNER, hip))
    c_plus = go(ccopy(r, C_PLUS, yp))
    c_minus = go(ccopy(r, C_MINUS, ym))
    c_far = go(ccopy(r, C_FAR, yy2))
    totals = []
    for d in range(1, 8):
        totals.append(small_copy(small.at[0], small_in.at[d], d, ((r + d) % 8, c)))
        totals[-1].start()

    prepare(3, 11)
    rg[...] = jnp.zeros_like(rg)
    lacc[...] = jnp.zeros_like(lacc)
    slopes_b[...] = jnp.zeros_like(slopes_b)
    cg[...] = jnp.zeros_like(cg)

    r_partner.wait_recv()
    r_pplus = go(rcopy(1 - lo, z, R_PPLUS, zp))
    r_pminus = go(rcopy(1 - lo, z, R_PMINUS, zm))
    r_pfar = go(rcopy(1 - lo, z, R_PFAR, zz2))
    prepare(11, 14)
    r_plus.wait_recv()
    r_minus.wait_recv()
    r_far.wait_recv()
    r_sib = go(remote(rows.at[lo, :, core], rows.at[lo, :, core], R_SIB, sib))
    prepare(14, 16)
    c_partner.wait_recv()
    c_pplus = go(ccopy(qh, C_PPLUS, yp))
    c_pminus = go(ccopy(qh, C_PMINUS, ym))

    c_pfar = ccopy(rf, C_PFAR, hip)
    r_psib = remote(rows.at[1 - lo, :, core], rows.at[1 - lo, :, core], R_PSIB, sib)

    grand = small[0]
    for d in range(1, 8):
        totals[d - 1].wait_recv()
        grand = grand + small_in[d]
    log_total = jnp.log(grand[0:1, 0:1])

    def turn_rows(l):
        for zz in range(4):
            for k in range(2):
                at = pl.ds(pl.multiple_of(l * 1024 + (zz * 2 + k) * 128, 128), 128)
                rowsT[:, at] = jnp.transpose(rows[l, zz, k].astype(F32)).astype(BF16)

    r_sib.wait_recv()
    turn_rows(lo)

    def piece(conf, score, base):
        x = score - base
        t = conf * x
        g = jnp.exp2(jnp.where(conf > 0, -1e4, x) * LOG2E)
        d = g + 2.0 ** -SHIFT
        slope = (t + g * pltpu.reciprocal(d, approx=True)).astype(BF16)
        fold = (PIECE // 8, 8, 256)
        return slope, jnp.sum((t * x).reshape(fold), axis=0), jnp.sum(jnp.log2(d).reshape(fold), axis=0)

    def kind_of(u):
        return jnp.where((u == 0) | (u == 3), CROSS, jnp.where((u == 1) | (u == 2), FAR, jnp.where(u <= 6, u - 4, 5 + (u - 7) // 2)))

    def plane_of(u):
        return jnp.where((u <= 1) | ((u >= 8) & (u % 2 == 0)), lo, 1 - lo)

    def block_of(kind):
        off = jnp.where((kind == NEXT) | (kind == CROSS_NEXT), 1, jnp.where(
            (kind == LAST) | (kind == CROSS_LAST), 3, jnp.where((kind == FAR) | (kind == CROSS_FAR), 2, 0)))
        h = jnp.where((kind <= LAST) | (kind == FAR), hi, 1 - hi)
        return h * 4 + (y + off) % 4

    def row_base(l, q):
        return pl.multiple_of(l * 1024 + q * TILE, TILE)

    def do_scores(dst, l, q, blk):
        tile = rows[l, 2 * q:2 * q + 2].reshape(TILE, K)
        dst[...] = lax.dot_general(
            tile, cols[blk], (((1,), (1,)), ((), ())), preferred_element_type=F32) - log_total

    def elementwise(src, dst, l, q, c0):
        la = jnp.zeros((8, 256), F32)
        lb = jnp.zeros((8, 256), F32)
        for v in range(TILE // PIECE):
            at = slice(v * PIECE, (v + 1) * PIECE)
            ra = pl.ds(pl.multiple_of(l * 1024 + q * TILE + v * PIECE, PIECE), PIECE)
            dst[at], a, b = piece(C[ra, pl.ds(c0, 256)], src[at], B[ra, pl.ds(c0, 256)])
            la = la + a
            lb = lb + b
        lacc[...] += la * 0.5 + (lb + float(SHIFT * TILE // 8)) * LN2

    def gradients(src, l, q, blk, kind):
        at = pl.ds(row_base(l, q), TILE)
        rg[at, :] += jnp.dot(src[...], cols[blk], preferred_element_type=F32)
        cg[kind] += jnp.dot(rowsT[:, at], src[...], preferred_element_type=F32)

    S_FAR, S_NEXT_RELAY, S_LAST_RELAY, S_CROSS_FAR, S_CROSS, S_NEXT, S_LAST = range(7)
    col_dest = [rf, row_at(hi, y + 1), row_at(hi, y - 1), row_at(1 - hi, y + 2), qh, row_at(hi, y + 1), row_at(hi, y - 1)]

    def col_copy(j):
        return remote(csend.at[j], cpart.at[j], G_COLS + j, (col_dest[j], c))

    def send_cols(j, value):
        csend[j] = value.astype(BF16)
        col_copy(j).start()

    OFFS = (2, 1, 3, 0)

    def rg_block(l, off, k):
        p = l * 4 + (z + off) % 4
        return rg[pl.ds(pl.multiple_of((p * 2 + k) * 128, 128), 128), :]

    sib_batch = remote(rsend.at[0:4], rsib.at[0:4], G_SIB, sib)

    def sib_copy(i):
        return remote(rsend.at[i], rsib.at[i], G_SIB + i, sib)

    def row_copy(i):
        l = 1 - lo if i in (0, 3) else lo
        dev = (r, col_at(l, z + OFFS[i % 4], core))
        return remote(rsum.at[i], rpart.at[i], G_ROWS + i, dev)

    def send_rows(i, value):
        rsum[i] = value.astype(BF16)
        row_copy(i).start()

    def at_step(u):
        return plane_of(u), block_of(kind_of(u)), kind_of(u)

    def tile_scores(dst, u, q):
        l, blk, _ = at_step(u)
        do_scores(dst, l, q, blk)

    def tile_slopes(src, dst, u, q):
        l, blk, _ = at_step(u)
        elementwise(src, dst, l, q, pl.multiple_of(blk * 256, 256))

    def tile_gradients(src, u, q):
        l, blk, kind = at_step(u)
        gradients(src, l, q, blk, kind)

    c_far.wait_recv()
    c_pfar.start()
    r_pplus.wait_recv()
    r_pminus.wait_recv()
    r_pfar.wait_recv()
    r_psib.start()
    tile_scores(scores_a, 0, 0)
    tile_scores(scores_b, 0, 1)
    tile_slopes(scores_a, slopes_a, 0, 0)
    tile_scores(scores_a, 1, 0)
    tile_slopes(scores_b, slopes_b, 0, 1)
    tile_gradients(slopes_a, 0, 0)
    tile_scores(scores_b, 1, 1)
    tile_slopes(scores_a, slopes_a, 1, 0)
    tile_gradients(slopes_b, 0, 1)
    tile_slopes(scores_b, slopes_b, 1, 1)
    tile_gradients(slopes_a, 1, 0)
    r_psib.wait_recv()
    c_plus.wait_recv()
    c_minus.wait_recv()
    turn_rows(1 - lo)
    tile_scores(scores_a, 2, 0)

    def run_if(test):
        return (lambda body: body()) if test else (lambda body: None)

    def steps(m, carry):
        u = m * 2

        @run_if(m == 2)
        def _():
            send_cols(S_FAR, cg[FAR])

        @run_if(m == 3)
        def _():
            c_pminus.wait_recv()

        @run_if(m == 4)
        def _():
            c_pplus.wait_recv()

        @run_if(m == 5)
        def _():
            send_cols(S_NEXT_RELAY, cg[CROSS_NEXT])
            c_pfar.wait_recv()

        tile_scores(scores_b, u, 1)
        tile_slopes(scores_a, slopes_a, u, 0)
        tile_gradients(slopes_b, u - 1, 1)
        tile_scores(scores_a, u + 1, 0)
        tile_slopes(scores_b, slopes_b, u, 1)
        tile_gradients(slopes_a, u, 0)
        tile_scores(scores_b, u + 1, 1)
        tile_slopes(scores_a, slopes_a, u + 1, 0)
        tile_gradients(slopes_b, u, 1)
        tile_scores(scores_a, u + 2, 0)
        tile_slopes(scores_b, slopes_b, u + 1, 1)
        tile_gradients(slopes_a, u + 1, 0)
        return carry

    for m in range(1, 6):
        steps(m, 0)

    send_cols(S_LAST_RELAY, cg[CROSS_LAST])
    tile_scores(scores_b, 12, 1)
    tile_slopes(scores_a, slopes_a, 12, 0)
    tile_gradients(slopes_b, 11, 1)
    for i in range(4):
        rsend[i] = rg_block(1 - lo, OFFS[i], 1 - core).astype(BF16)
    sib_batch.start()
    tile_slopes(scores_b, slopes_b, 12, 1)
    tile_gradients(slopes_a, 12, 0)

    qcols = [r, row_at(hi, y + 1), row_at(hi, y - 1)]
    for h in range(3):
        colsq[h * 256:(h + 1) * 256] = cols[qcols[h]]
        cgq[:, h * 256:(h + 1) * 256] = cg[h]

    def chip_of(t):
        off = jnp.where(t == 0, 2, jnp.where(t == 1, 1, jnp.where(t == 2, 3, 0)))
        return (z + off) % 4

    def q_rows(t, v, size):
        return pl.ds(pl.multiple_of(lo * 1024 + chip_of(t) * 256 + v, size), size)

    def q_scores(dst, t):
        tile = rows[lo, chip_of(t)].reshape(256, K)
        dst[...] = lax.dot_general(
            tile, colsq[...], (((1,), (1,)), ((), ())), preferred_element_type=F32) - log_total

    def q_elementwise(src, dst, t):
        la = jnp.zeros((8, 256), F32)
        lb = jnp.zeros((8, 256), F32)
        for h in range(3):
            c0 = pl.multiple_of(qcols[h] * 256, 256)
            for v in range(256 // PIECE):
                at = slice(v * PIECE, (v + 1) * PIECE)
                to = slice(h * 256, (h + 1) * 256)
                ra = q_rows(t, v * PIECE, PIECE)
                dst[at, to], a, b = piece(C[ra, pl.ds(c0, 256)], src[at, to], B[ra, pl.ds(c0, 256)])
                la = la + a
                lb = lb + b
        lacc[...] += la * 0.5 + (lb + float(SHIFT * WIDTH // 8)) * LN2

    def q_gradients(src, t):
        at = q_rows(t, 0, 256)
        rg[at, :] += jnp.dot(src[...], colsq[...], preferred_element_type=F32)
        cgq[...] += jnp.dot(rowsT[:, at], src[...], preferred_element_type=F32)

    def to_sibling(t):
        rsend[4 + t] = rg_block(lo, OFFS[t], 1 - core).astype(BF16)
        sib_copy(4 + t).start()

    def to_owner(t):
        sib_copy(4 + t).wait_recv()
        send_rows(4 + t, rg_block(lo, OFFS[t], core) + rsib[4 + t].astype(F32))

    tile_gradients(slopes_b, 12, 1)
    q_scores(sq_a, 0)
    send_cols(S_CROSS_FAR, cg[CROSS_FAR])
    sib_batch.wait_recv()
    for i in (1, 2, 0):
        send_rows(i, rg_block(1 - lo, OFFS[i], core) + rsib[i].astype(F32))

    q_scores(sq_b, 1)
    q_elementwise(sq_a, tq_a, 0)
    q_scores(sq_a, 2)
    q_elementwise(sq_b, tq_b, 1)
    q_gradients(tq_a, 0)
    to_sibling(0)
    q_scores(sq_b, 3)
    q_elementwise(sq_a, tq_a, 2)
    q_gradients(tq_b, 1)
    to_sibling(1)
    to_owner(0)
    q_elementwise(sq_b, tq_b, 3)
    q_gradients(tq_a, 2)
    to_sibling(2)
    to_owner(1)
    small[1] = jnp.broadcast_to(
        jnp.sum(jnp.sum(lacc[...], axis=0, keepdims=True), axis=1, keepdims=True), (8, 128))
    losses = []
    for d in range(1, 8):
        losses.append(small_copy(small.at[1], small_row.at[d], 7 + d, ((r + d) % 8, c)))
        losses[-1].start()
    q_gradients(tq_b, 3)
    send_cols(S_NEXT, cgq[:, 256:512])
    send_cols(S_LAST, cgq[:, 512:768])
    to_sibling(3)
    to_owner(2)

    col_copy(S_NEXT_RELAY).wait_recv()
    col_copy(S_LAST_RELAY).wait_recv()
    send_cols(S_CROSS, cg[CROSS] + cpart[S_NEXT_RELAY].astype(F32) + cpart[S_LAST_RELAY].astype(F32))
    grad = rg_block(1 - lo, 0, core) + rsib[3].astype(F32)
    for i in (1, 2):
        row_copy(i).wait_recv()
        grad = grad + rpart[i].astype(F32)
    send_rows(3, grad)

    loss = small[1]
    for d in range(1, 8):
        losses[d - 1].wait_recv()
        loss = loss + small_row[d]
    small[2] = loss
    for d in range(1, 16):
        losses.append(small_copy(small.at[2], small_col.at[d], 14 + d, (r, (c + d) % 16)))
        losses[-1].start()

    sib_copy(7).wait_recv()
    grad = rg_block(lo, 0, core) + rsib[7].astype(F32)
    for i in (4, 5, 6, 0):
        row_copy(i).wait_recv()
        grad = grad + rpart[i].astype(F32)
    total = cgq[:, 0:256]
    for j in (S_FAR, S_NEXT, S_LAST, S_CROSS_FAR, S_CROSS):
        col_copy(j).wait_recv()
        total = total + cpart[j].astype(F32)
    column_grad[...] = jnp.transpose(total)
    row_copy(3).wait_recv()
    row_grad[...] = grad + rpart[3].astype(F32)

    loss = small[2]
    for d in range(1, 16):
        losses[6 + d].wait_recv()
        loss = loss + small_col[d]
    mean_loss[...] = loss * (1.0 / 536870912.0)

    for copy in sent + totals + losses + [c_pfar, r_psib, sib_batch]:
        copy.wait_send()
    for j in range(7):
        col_copy(j).wait_send()
    for i in range(4, 8):
        sib_copy(i).wait_send()
    for i in range(7):
        row_copy(i).wait_send()


def update(
    row_grad, column_grad, loss, row_vectors, column_vectors, row_squares, column_squares,
    new_rows, new_columns, squares_row, squares_column, mean_loss,
):
    g = row_grad[...]
    s = row_squares[...] + g * g
    squares_row[...] = s
    new_rows[...] = row_vectors[...] - g * lax.rsqrt(s)
    g = column_grad[...]
    s = column_squares[...] + g * g
    squares_column[...] = s
    new_columns[...] = column_vectors[...] - g * lax.rsqrt(s)
    mean_loss[0, 0] = loss[0, 0]


def on_device(
    counts, row_totals, column_totals, row_vectors, column_vectors, row_squares, column_squares
):
    vmem = pl.BlockSpec(memory_space=pltpu.VMEM)
    smem = pl.BlockSpec(memory_space=pltpu.SMEM)
    row_grad, column_grad, loss = pl.pallas_call(
        kernel,
        out_shape=[
            jax.ShapeDtypeStruct((128, K), F32),
            jax.ShapeDtypeStruct((256, K), F32),
            jax.ShapeDtypeStruct((8, 128), F32),
        ],
        in_specs=[pl.BlockSpec(memory_space=pl.ANY)] * 5,
        out_specs=[vmem] * 3,
        scratch_shapes=[
            pltpu.VMEM((16, 128), jnp.int32),
            pltpu.VMEM((1, NC), jnp.int32),
            pltpu.VMEM((128, K), F32),
            pltpu.VMEM((256, K), F32),
            pltpu.VMEM((SLOTS, STRIP, NC), jnp.int32),
            pltpu.VMEM((NR, 128), F32),
            pltpu.VMEM((8, NC), F32),
            pltpu.VMEM((NR, NC), F32),
            pltpu.VMEM((NR, NC), F32),
            pltpu.VMEM((2, 4, 2, 128, K), BF16),
            pltpu.VMEM((K, NR), BF16),
            pltpu.VMEM((8, 256, K), BF16),
            pltpu.VMEM((WIDTH, K), BF16),
            pltpu.VMEM((NR, K), F32),
            pltpu.VMEM((8, K, 256), F32),
            pltpu.VMEM((K, WIDTH), F32),
            pltpu.VMEM((TILE, 256), BF16),
            pltpu.VMEM((TILE, 256), BF16),
            pltpu.VMEM((TILE, 256), F32),
            pltpu.VMEM((TILE, 256), F32),
            pltpu.VMEM((256, WIDTH), F32),
            pltpu.VMEM((256, WIDTH), F32),
            pltpu.VMEM((256, WIDTH), BF16),
            pltpu.VMEM((256, WIDTH), BF16),
            pltpu.VMEM((8, 256), F32),
            pltpu.VMEM((7, K, 256), BF16),
            pltpu.VMEM((7, K, 256), BF16),
            pltpu.VMEM((8, 128, K), BF16),
            pltpu.VMEM((8, 128, K), BF16),
            pltpu.VMEM((8, 128, K), BF16),
            pltpu.VMEM((8, 128, K), BF16),
            pltpu.VMEM((3, 8, 128), F32),
            pltpu.VMEM((8, 8, 128), F32),
            pltpu.VMEM((8, 8, 128), F32),
            pltpu.VMEM((16, 8, 128), F32),
            pltpu.SemaphoreType.DMA((SLOTS,)),
            pltpu.SemaphoreType.DMA((4,)),
            pltpu.SemaphoreType.DMA((N_SEMS,)),
            pltpu.SemaphoreType.DMA((N_SEMS,)),
            pltpu.SemaphoreType.DMA((32,)),
            pltpu.SemaphoreType.DMA((32,)),
        ],
        compiler_params=pltpu.CompilerParams(
            collective_id=0, has_side_effects=True, vmem_limit_bytes=63 * 1024 * 1024),
        name="swivel_step",
    )(counts, row_totals.reshape(16, 128), column_totals.reshape(1, NC), row_vectors, column_vectors)
    outs = pl.pallas_call(
        update,
        out_shape=[
            jax.ShapeDtypeStruct((128, K), F32),
            jax.ShapeDtypeStruct((256, K), F32),
            jax.ShapeDtypeStruct((128, K), F32),
            jax.ShapeDtypeStruct((256, K), F32),
            jax.ShapeDtypeStruct((1, 1), F32),
        ],
        in_specs=[vmem, vmem, smem] + [vmem] * 4,
        out_specs=[vmem] * 4 + [smem],
        name="adagrad_update",
    )(row_grad, column_grad, loss, row_vectors, column_vectors, row_squares, column_squares)
    return outs[0], outs[1], outs[2], outs[3], outs[4].reshape(())


def solution(mesh):
    in_specs = (
        P("row", "col"),
        P("row"),
        P("col"),
        P(("row", "col"), None),
        P(("col", "row"), None),
        P(("row", "col"), None),
        P(("col", "row"), None),
    )
    out_specs = (
        P(("row", "col"), None),
        P(("col", "row"), None),
        P(("row", "col"), None),
        P(("col", "row"), None),
        P(),
    )
    return jax.shard_map(
        on_device, mesh=mesh, in_specs=in_specs, out_specs=out_specs, check_vma=False
    )
```
